32 devices in a mesh: strip: 8 (over z, y), sub: 4 (over x, core).
Axes of the slice: x: 2, y: 2, z: 4, core: 2. Of those that a mesh axis runs over, the one named last changes fastest.
Arguments:
- currents: bfloat16 [32, 64, 32, 128], P('strip', 'sub'), may hold values from -6 to 6
- near_blocks: bfloat16 [32, 64, 9, 1024], P('strip', 'sub'), may hold values from -0.375 to 0.375
- near_index: int32 [32, 64, 9], P('strip', 'sub'), may hold values from -1 to 2047, as said below
- box_of_patch: int32 [32, 64], P('strip', 'sub'), may hold values from 0 to 255, as said below
- box_centre: float32 [256, 2], P(('strip', 'sub')), as said below
- patch_angle: float32 [32, 64, 128], P('strip', 'sub'), may hold values from -3.140625 to 3.140625
- aggregation: bfloat16 [2, 128, 32], replicated, may hold values from -1 to 1
- disaggregation: bfloat16 [2, 128, 32], replicated, may hold values from -0.375 to 0.375
- strip_shift: float32 [8, 2, 128], P('strip'), may hold values from -1 to 1, as said below
Outputs:
- operator_image: bfloat16 [32, 64, 32, 128], P('strip', 'sub')
The draws below stay inside these ranges and needn't reach their ends.
Inputs may be any that keep to these rules, and one draw needn't show every extreme that they name: `near_index`: each patch's list holds ids of distinct patches that lie within one row and one column of it, the patch itself always among them, listed entries first and -1 in the remaining slots; some lists are full. `box_of_patch`: the patches of device block (i, j), rows i * 4 to (i + 1) * 4 - 1 and columns j * 16 to (j + 1) * 16 - 1, name only boxes (i * 4 + j) * 8 to (i * 4 + j + 1) * 8 - 1, each exactly 8 times. `box_centre`: box b with b // 8 = i * 4 + j has its centre in [i * 4, (i + 1) * 4] x [j * 16, (j + 1) * 16]. `strip_shift`: every translation has magnitude at most 1.
All inputs are finite; a program needn't handle non-finite values.
Results may differ from the reference program's by a relative error of at most 0.009.
Values may be sent and summed in bfloat16 or wider, within the bound.
A program may use at most 128 MiB of HBM per device.

```python
import math
import jax
import jax.numpy as jnp
from jax import lax

CX = 4
CY = 16
U = 32
R = 128
KC = 128
NB = 9
PER_BOX = 8
BAND_TOTAL = 8
NSUBS = 4
NX = 32
NY = 64
BOX_DEV = 8
BOX_STRIP = 32
BOXES = 256


def draw_near_index(key, part):
    offsets = jnp.arange(NB, dtype=jnp.int32)
    off_x = offsets // 3 - 1
    off_y = offsets % 3 - 1
    grid_x = jnp.arange(NX, dtype=jnp.int32)[:, None, None]
    grid_y = jnp.arange(NY, dtype=jnp.int32)[None, :, None]
    kept = jax.random.randint(key, (NX, NY, NB), 0, 10) < 7
    forced = (grid_x % CX == 1) & (grid_y % CY == 1)
    kept = kept | (offsets == 4) | forced
    near_x = grid_x + off_x
    near_y = grid_y + off_y
    inside = (near_x >= 0) & (near_x < NX) & (near_y >= 0) & (near_y < NY)
    usable = jnp.broadcast_to(kept & inside, (NX, NY, NB))
    score = jnp.where(usable, 0, 16) + offsets
    order = jnp.argsort(score, axis=2, stable=True)
    patch_ids = jnp.broadcast_to(near_x * NY + near_y, (NX, NY, NB))
    sorted_ids = jnp.take_along_axis(patch_ids, order, axis=2)
    sorted_use = jnp.take_along_axis(usable, order, axis=2)
    return jnp.where(sorted_use, sorted_ids, -1).astype(jnp.int32)


def draw_box_of_patch(key, part):
    per_device = CX * CY
    block_count = BAND_TOTAL * NSUBS
    noise = jax.random.randint(key, (block_count, per_device), 0, 1 << 20) * per_device
    noise = noise + jnp.arange(per_device, dtype=jnp.int32)[None, :]
    ranking = jnp.argsort(jnp.argsort(noise, axis=1), axis=1).astype(jnp.int32)
    local_box = ranking // PER_BOX + (jnp.arange(block_count, dtype=jnp.int32) * BOX_DEV)[:, None]
    shaped = local_box.reshape(BAND_TOTAL, NSUBS, CX, CY).transpose(0, 2, 1, 3)
    return shaped.reshape(NX, NY).astype(jnp.int32)


def draw_box_centre(key, part):
    row_block = jnp.arange(BOXES, dtype=jnp.int32) // BOX_DEV
    strip_at = (row_block // NSUBS).astype(jnp.float32)
    sub_at = (row_block % NSUBS).astype(jnp.float32)
    low_edge, high_edge = (0.1, 0.9)
    spots = jax.random.uniform(key, (BOXES, 2), jnp.float32, low_edge, high_edge)
    return jnp.stack([(strip_at + spots[:, 0]) * CX, (sub_at + spots[:, 1]) * CY], axis=1)


def draw_strip_shift(key, part):
    frequency_seed, perturbation_seed, spell_seed, spin_seed = jax.random.split(key, 4)
    low_rate, high_rate = (0.1, 30.0)
    incoming_frequencies = jnp.exp(jax.random.uniform(frequency_seed, (1, KC), jnp.float32, math.log(low_rate), math.log(high_rate))) / BAND_TOTAL
    stochastic_perturbation = jax.random.uniform(perturbation_seed, (BAND_TOTAL, KC), jnp.float32, 0.5, 1.5)
    spell_durations = jnp.where(jax.random.randint(spell_seed, (BAND_TOTAL, 1), 0, 16) == 0, 0.8, 1.0).astype(jnp.float32)
    excitation_strength = jnp.exp(-incoming_frequencies * stochastic_perturbation) * spell_durations
    turns = jax.random.uniform(spin_seed, (BAND_TOTAL, KC), jnp.float32, -math.pi, math.pi)
    return jnp.stack([excitation_strength * jnp.cos(turns), excitation_strength * jnp.sin(turns)], axis=1)


def shard_levels(stream_key, extent, cuts, low, largest):
    factor_of, own = 1.0, jax.random.fold_in(stream_key, 6)
    for position, parts in cuts:
        steps = jnp.exp(jax.random.uniform(jax.random.fold_in(own, position), (parts,), jnp.float32, low / len(cuts), largest / len(cuts)))
        factor_of = factor_of * jnp.repeat(steps, extent[position] // parts).reshape([-1 if axis == position else 1 for axis in range(len(extent))])
    return factor_of


def bell_draw(rng, dims, deviation, bound, pieces=(), held_as=jnp.bfloat16):
    factor_of = shard_levels(rng, dims, pieces, -0.22, 0.18) if pieces else 1.0
    values = jax.random.normal(rng, dims, jnp.float32) * deviation * factor_of
    return jnp.minimum(jnp.maximum(values, -bound), bound).astype(held_as)


def setup_inputs(seed: int = 0) -> dict:
    keys = jax.random.split(jax.random.key(seed), 10)
    return {
        "currents": bell_draw(keys[0], (NX, NY, U, R), 1.0, 6.0, ((0, 8), (1, 4))),
        "near_blocks": bell_draw(keys[1], (NX, NY, NB, U * U), (U * NB) ** -0.5, 0.375, ((0, 8), (1, 4))),
        "near_index": draw_near_index(jax.random.fold_in(keys[9], 71), 0),
        "box_of_patch": draw_box_of_patch(jax.random.fold_in(keys[9], 71), 0),
        "box_centre": draw_box_centre(jax.random.fold_in(keys[9], 71), 0),
        "patch_angle": jnp.clip(jax.random.uniform(keys[5], (NX, NY, KC), jnp.float32, -3.140625, 3.140625), -3.140625, 3.140625),
        "aggregation": bell_draw(keys[6], (2, KC, U), U ** -0.5, 1.0),
        "disaggregation": bell_draw(keys[7], (2, KC, U), (2 * KC) ** -0.5, 0.375),
        "strip_shift": draw_strip_shift(jax.random.fold_in(keys[9], 71), 0),
    }


wave_number = 1.5
strip_weight = 0.03

def rounded(values):
    return lax.optimization_barrier(values.astype(jnp.bfloat16)).astype(jnp.float32)

def directions():
    angles = 2.0 * math.pi / KC * jnp.arange(KC, dtype=jnp.float32)
    return (jnp.cos(angles), jnp.sin(angles))

def centre_phase(centre, strip_id):
    dir_x, dir_y = directions()
    centre_x = (strip_id.astype(jnp.float32) + 0.5) * CX
    centre_y = 0.5 * NY
    phase_arg = wave_number * ((centre[:, 0:1] - centre_x) * dir_x + (centre[:, 1:2] - centre_y) * dir_y)
    return (jnp.cos(phase_arg), jnp.sin(phase_arg))

def pair_weights(target_centre, source_centre, target_ids, source_ids):
    dir_x, dir_y = directions()
    delta_x = target_centre[:, None, 0] - source_centre[None, :, 0]
    delta_y = target_centre[:, None, 1] - source_centre[None, :, 1]
    distance = jnp.sqrt(delta_x * delta_x + delta_y * delta_y)
    amplitude = jnp.where(target_ids[:, None] != source_ids[None, :], 1.0 / (1.0 + distance), 0.0)
    phase_arg = wave_number * (distance[:, :, None] + delta_x[:, :, None] * dir_x + delta_y[:, :, None] * dir_y)
    return (rounded(amplitude[:, :, None] * jnp.cos(phase_arg)), rounded(amplitude[:, :, None] * jnp.sin(phase_arg)))

def complex_scale(gain_re, gain_im, values):
    real_part = gain_re[:, None] * values[0] - gain_im[:, None] * values[1]
    imag_part = gain_re[:, None] * values[1] + gain_im[:, None] * values[0]
    return jnp.stack([real_part, imag_part])

def reference(currents, near_blocks, near_index, box_of_patch, box_centre, patch_angle, aggregation, disaggregation, strip_shift):
    strip_patches = CX * NY
    agg_wide = aggregation.astype(jnp.float32)
    dis_wide = disaggregation.astype(jnp.float32)

    def gather_boxes(strip_id):
        strip_rows = lax.dynamic_slice_in_dim(currents, strip_id * CX, CX, 0).reshape(strip_patches, U, R).astype(jnp.float32)
        wave_part = jnp.einsum('ckv,pvr->pckr', agg_wide, strip_rows)
        patch_turn = lax.dynamic_slice_in_dim(patch_angle, strip_id * CX, CX, 0).reshape(strip_patches, KC)
        cosine = jnp.cos(patch_turn)[:, :, None]
        sine_part = jnp.sin(patch_turn)[:, :, None]
        turned = jnp.stack([cosine * wave_part[:, 0] - sine_part * wave_part[:, 1], sine_part * wave_part[:, 0] + cosine * wave_part[:, 1]], axis=1)
        owner_box = lax.dynamic_slice_in_dim(box_of_patch, strip_id * CX, CX, 0).reshape(strip_patches) - strip_id * BOX_STRIP
        box_values = jax.ops.segment_sum(turned, owner_box, num_segments=BOX_STRIP).astype(jnp.bfloat16)
        centre = lax.dynamic_slice_in_dim(box_centre, strip_id * BOX_STRIP, BOX_STRIP, 0)
        phase_re, phase_im = centre_phase(centre, strip_id)
        box_wide = lax.optimization_barrier(box_values).astype(jnp.float32)
        sum_re = lax.optimization_barrier(jnp.sum(phase_re[:, :, None] * box_wide[:, 0] - phase_im[:, :, None] * box_wide[:, 1], axis=0))
        sum_im = lax.optimization_barrier(jnp.sum(phase_im[:, :, None] * box_wide[:, 0] + phase_re[:, :, None] * box_wide[:, 1], axis=0))
        return (box_values, strip_weight * jnp.stack([sum_re, sum_im]))
    all_boxes, expansions = lax.map(gather_boxes, jnp.arange(BAND_TOTAL, dtype=jnp.int32))

    def advance(carried, element):
        exp_item, gain_re, gain_im = element
        moved = complex_scale(gain_re, gain_im, carried)
        return (exp_item + moved, moved)
    empty_field = jnp.zeros((2, KC, R), jnp.float32)
    _, upward = lax.scan(advance, empty_field, (expansions, strip_shift[:, 0], strip_shift[:, 1]))
    _, downward = lax.scan(advance, empty_field, (expansions, strip_shift[:, 0], -strip_shift[:, 1]), reverse=True)
    strip_field = upward + downward
    flat_currents = currents.reshape(NX * NY, U, R)

    def apply_strip(strip_id):
        box_wide = all_boxes[strip_id].astype(jnp.float32)
        centre = lax.dynamic_slice_in_dim(box_centre, strip_id * BOX_STRIP, BOX_STRIP, 0)
        box_ids = jnp.arange(BOX_STRIP, dtype=jnp.int32)
        weight_re, weight_im = pair_weights(centre, centre, box_ids, box_ids)
        source_re = box_wide[:, 0]
        source_im = box_wide[:, 1]
        in_re = jnp.einsum('tsk,skr->tkr', weight_re, source_re) - jnp.einsum('tsk,skr->tkr', weight_im, source_im)
        in_im = jnp.einsum('tsk,skr->tkr', weight_re, source_im) + jnp.einsum('tsk,skr->tkr', weight_im, source_re)
        phase_re, phase_im = centre_phase(centre, strip_id)
        here = strip_field[strip_id]
        local_re = in_re + phase_re[:, :, None] * here[0] + phase_im[:, :, None] * here[1]
        local_im = in_im + phase_re[:, :, None] * here[1] - phase_im[:, :, None] * here[0]
        owner_box = lax.dynamic_slice_in_dim(box_of_patch, strip_id * CX, CX, 0).reshape(strip_patches) - strip_id * BOX_STRIP
        patch_re = local_re[owner_box]
        patch_im = local_im[owner_box]
        patch_turn = lax.dynamic_slice_in_dim(patch_angle, strip_id * CX, CX, 0).reshape(strip_patches, KC)
        cosine = jnp.cos(patch_turn)[:, :, None]
        sine_part = jnp.sin(patch_turn)[:, :, None]
        received = rounded(jnp.stack([cosine * patch_re + sine_part * patch_im, cosine * patch_im - sine_part * patch_re], axis=1))
        far_sum = jnp.einsum('ckv,pckr->pvr', dis_wide, received)
        index_rows = lax.dynamic_slice_in_dim(near_index, strip_id * CX, CX, 0).reshape(strip_patches, NB)
        block_rows = lax.dynamic_slice_in_dim(near_blocks, strip_id * CX, CX, 0).reshape(strip_patches, NB, U, U).astype(jnp.float32)
        near_sum = jnp.zeros((strip_patches, U, R), jnp.float32)
        for slot_id in range(NB):
            picked = index_rows[:, slot_id]
            fetched = jnp.take(flat_currents, jnp.maximum(picked, 0), axis=0).astype(jnp.float32)
            fetched = fetched * (picked >= 0).astype(jnp.float32)[:, None, None]
            near_sum = near_sum + jnp.einsum('puv,pvr->pur', block_rows[:, slot_id], fetched)
        return (near_sum + far_sum).astype(jnp.bfloat16).reshape(CX, NY, U, R)
    result = lax.map(apply_strip, jnp.arange(BAND_TOTAL, dtype=jnp.int32))
    return result.reshape(NX, NY, U, R)
```

```python
import functools
import math

import jax
import jax.numpy as jnp
from jax import lax
from jax.experimental import pallas as pl
from jax.experimental.pallas import tpu as pltpu
from jax.sharding import PartitionSpec as P

wave_number = 1.5
strip_weight = 0.03
MESH = pl.DeviceIdType.MESH
f32 = jnp.float32
bf16 = jnp.bfloat16


def gather_boxes(perm_ref, cur_ref, angle_ref, agg_ref, box_ref, cos_ref, sin_ref, x_ref, e_ref):
    n_sub, n_box, _, quarter, _ = box_ref.shape
    n_patch, n_dirs = angle_ref.shape
    n_units = cur_ref.shape[1]
    per_box = n_patch // n_box
    cos_ref[...] = jnp.cos(angle_ref[...])
    sin_ref[...] = jnp.sin(angle_ref[...])

    def one_box(b, carry):
        agg_re, agg_im = agg_ref[0], agg_ref[1]
        for i in range(per_box):
            p = perm_ref[b * per_box + i]
            rows = slice(i * n_units, (i + 1) * n_units)
            x_ref[rows, :] = cur_ref[p]
            c = cos_ref[pl.ds(p, 1), :]
            s = sin_ref[pl.ds(p, 1), :]
            e_ref[rows, 0:n_dirs] = (c * agg_re - s * agg_im).astype(bf16)
            e_ref[rows, n_dirs : 2 * n_dirs] = (s * agg_re + c * agg_im).astype(bf16)
        values = lax.dot_general(
            e_ref[...], x_ref[...], (((0,), (0,)), ((), ())), preferred_element_type=f32
        ).astype(bf16)
        for c in range(2):
            for q in range(n_sub):
                at = c * n_dirs + q * quarter
                box_ref[q, b, c] = values[at : at + quarter]
        return carry

    lax.fori_loop(0, n_box, one_box, 0)


def near_part(located_ref, nb_ref, pad_ref, near_ref, a_ref, x_ref):
    n_patch, n_slots, _ = nb_ref.shape
    n_units, n_sides = near_ref.shape[1:]
    lanes = lax.broadcasted_iota(jnp.int32, (8, 128), 1) // 32

    def pick(parts):
        out = parts[0]
        for i in range(1, 4):
            out = jnp.where(lanes == i, parts[i], out)
        return out

    def one_patch(p, carry):
        for q in range(8):
            a_ref[q * 16 : q * 16 + n_slots, :] = nb_ref[p, :, q * 128 : (q + 1) * 128].astype(f32)
        for j in range(n_slots):
            x_ref[j * n_units : (j + 1) * n_units, :] = pad_ref[located_ref[p * n_slots + j]]
        flat = [a_ref[pl.ds(j, 8, stride=16), :] for j in range(n_slots)]
        lhs = []
        for g in range(2):
            group = flat[g * 4 : g * 4 + 4]
            rolled = []
            for d in range(4):
                mixed = pick([group[(u + d) % 4] for u in range(4)])
                rolled.append(mixed if d == 0 else pltpu.roll(mixed, 32 * d, 1))
            lhs.append(
                jnp.concatenate([pick([rolled[(j - u) % 4] for j in range(4)]) for u in range(4)], axis=0)
            )
        last = jnp.concatenate(
            [flat[8]] + [pltpu.roll(flat[8], 128 - 32 * u, 1) for u in range(1, 4)], axis=0
        )
        total = jnp.dot(
            jnp.concatenate(lhs, axis=1).astype(bf16), x_ref[0:256, :], preferred_element_type=f32
        )
        total += jnp.dot(
            last[:, 0:n_units].astype(bf16), x_ref[256 : 256 + n_units, :], preferred_element_type=f32
        )
        for u in range(4):
            near_ref[p, pl.ds(u, 8, stride=4), :] = total[u * 8 : u * 8 + 8]
        return carry

    lax.fori_loop(0, n_patch, one_patch, 0)


def far_part(perm_ref, slot_ref, lf_ref, dis_ref, cos_ref, sin_ref, near_ref, out_ref, d_ref, far_ref):
    n_sub, n_box, _, quarter, n_sides = lf_ref.shape
    n_patch, n_dirs = cos_ref.shape
    n_units = near_ref.shape[1]
    per_box = n_patch // n_box

    def one_box(b, carry):
        dis_re, dis_im = dis_ref[0], dis_ref[1]
        for i in range(per_box):
            p = perm_ref[b * per_box + i]
            rows = slice(i * n_units, (i + 1) * n_units)
            c = cos_ref[pl.ds(p, 1), :]
            s = sin_ref[pl.ds(p, 1), :]
            d_ref[rows, 0:n_dirs] = (c * dis_re - s * dis_im).astype(bf16)
            d_ref[rows, n_dirs : 2 * n_dirs] = (s * dis_re + c * dis_im).astype(bf16)
        field = jnp.concatenate([lf_ref[q, b, c] for c in range(2) for q in range(n_sub)], axis=0)
        far = jnp.dot(d_ref[...], field, preferred_element_type=f32)
        for i in range(per_box):
            far_ref[b * per_box + i] = far[i * n_units : (i + 1) * n_units]
        return carry

    lax.fori_loop(0, n_box, one_box, 0)

    def one_patch(p, carry):
        out_ref[p] = (near_ref[p] + far_ref[slot_ref[p]]).astype(bf16)
        return carry

    lax.fori_loop(0, n_patch, one_patch, 0)


def fused(
    n_strip, n_sub,
    perm_ref, slot_ref, located_ref, cur_ref, nb_ref, angle_ref, agg_ref, dis_ref, centre_ref, shift_ref,
    out_ref,
    pad_ref, box_ref, cos_ref, sin_ref, x_ref, e_ref, near_ref, a_ref, far_ref, lf_ref,
    cen_ref, shf_ref, in_ref, wide_ref, w_ref, inc_ref, exp_ref, coef_ref, send_ref,
    halo_send, halo_recv, cen_send, cen_recv, shf_send, shf_recv, a2a_send, a2a_recv,
    exp_send, exp_recv, back_send, back_recv,
):
    strip = lax.axis_index("strip")
    sub = lax.axis_index("sub")
    rows_x, rows_y = 4, 16
    rows_x, rows_y = cur_ref.shape[0], cur_ref.shape[1]
    n_units, n_sides = cur_ref.shape[2], cur_ref.shape[3]
    n_patch = rows_x * rows_y
    n_dirs = angle_ref.shape[1]
    quarter = n_dirs // n_sub
    n_box = centre_ref.shape[0]
    all_box = n_box * n_sub
    wide_y = rows_y + 2

    def sub_peer(d):
        return lax.rem(sub + d, n_sub)

    def strip_peer(d):
        return lax.rem(strip + d, n_strip)

    offsets = [(dx, dy) for dx in (-1, 0, 1) for dy in (-1, 0, 1) if dx or dy]

    barrier = pltpu.get_barrier_semaphore()
    for dx in (-1, 1):
        for dy in (-1, 1):
            pl.semaphore_signal(
                barrier, inc=1, device_id=(strip_peer(dx + n_strip), sub_peer(dy + n_sub)), device_id_type=MESH
            )
    for d in range(1, n_sub):
        pl.semaphore_signal(barrier, inc=1, device_id=(strip, sub_peer(d)), device_id_type=MESH)

    def greet(d, carry):
        pl.semaphore_signal(barrier, inc=1, device_id=(strip_peer(d), sub), device_id_type=MESH)
        return carry

    lax.fori_loop(1, n_strip, greet, 0)

    cen_ref[sub] = jnp.zeros((n_box, 128), f32)
    cen_ref[sub, :, 0:2] = centre_ref[...]
    shf_ref[strip] = jnp.zeros((8, n_dirs), f32)
    shf_ref[strip, 0:2, :] = shift_ref[0]
    pl.semaphore_wait(barrier, 4 + n_sub - 1 + n_strip - 1)

    def cen_copy(d):
        return pltpu.make_async_remote_copy(
            src_ref=cen_ref.at[sub], dst_ref=cen_ref.at[sub],
            send_sem=cen_send.at[d], recv_sem=cen_recv.at[d],
            device_id=(strip, sub_peer(d)), device_id_type=MESH,
        )

    def cen_wait(d):
        src = lax.rem(sub + n_sub - d, n_sub)
        return pltpu.make_async_remote_copy(
            src_ref=cen_ref.at[src], dst_ref=cen_ref.at[src],
            send_sem=cen_send.at[d], recv_sem=cen_recv.at[d],
            device_id=(strip, sub_peer(d)), device_id_type=MESH,
        )

    def strip_copy(buf, send, recv, d, at):
        return pltpu.make_async_remote_copy(
            src_ref=buf.at[at], dst_ref=buf.at[at],
            send_sem=send.at[d], recv_sem=recv.at[d],
            device_id=(strip_peer(d), sub), device_id_type=MESH,
        )

    def halo_copy(n):
        dx, dy = offsets[n]
        src_x = {-1: slice(0, 1), 0: slice(0, rows_x), 1: slice(rows_x - 1, rows_x)}[dx]
        src_y = {-1: slice(0, 1), 0: slice(0, rows_y), 1: slice(rows_y - 1, rows_y)}[dy]
        dst_x = {-1: slice(rows_x + 1, rows_x + 2), 0: slice(1, rows_x + 1), 1: slice(0, 1)}[dx]
        dst_y = {-1: slice(rows_y + 1, rows_y + 2), 0: slice(1, rows_y + 1), 1: slice(0, 1)}[dy]
        return pltpu.make_async_remote_copy(
            src_ref=cur_ref.at[src_x, src_y], dst_ref=pad_ref.at[dst_x, dst_y],
            send_sem=halo_send.at[n], recv_sem=halo_recv.at[n],
            device_id=(strip_peer(dx + n_strip), sub_peer(dy + n_sub)), device_id_type=MESH,
        )

    for d in range(1, n_sub):
        cen_copy(d).start()

    def send_shift(d, carry):
        strip_copy(shf_ref, shf_send, shf_recv, d, strip).start()
        return carry

    lax.fori_loop(1, n_strip, send_shift, 0)
    for n in range(len(offsets)):
        halo_copy(n).start()

    flat_cur = cur_ref.reshape(n_patch, n_units, n_sides)
    flat_pad = pad_ref.reshape((rows_x + 3) * wide_y, n_units, n_sides)

    gather_boxes(perm_ref, flat_cur, angle_ref, agg_ref, box_ref, cos_ref, sin_ref, x_ref.at[0:256], e_ref)

    def a2a_copy(d):
        return pltpu.make_async_remote_copy(
            src_ref=box_ref.at[sub_peer(d)], dst_ref=in_ref.at[d],
            send_sem=a2a_send.at[d], recv_sem=a2a_recv.at[d],
            device_id=(strip, sub_peer(d)), device_id_type=MESH,
        )

    for d in range(1, n_sub):
        a2a_copy(d).start()

    for x in range(rows_x):
        pad_ref[x + 1, 1 : rows_y + 1] = cur_ref[x]
    pad_ref[rows_x + 2, 0] = jnp.zeros((n_units, n_sides), bf16)

    def wait_shift(d, carry):
        src = lax.rem(strip + n_strip - d, n_strip)
        strip_copy(shf_ref, shf_send, shf_recv, d, src).wait_recv()
        return carry

    lax.fori_loop(1, n_strip, wait_shift, 0)
    for d in range(1, n_sub):
        cen_wait(d).wait_recv()
    one = jnp.ones((1, n_dirs), f32)
    zero = jnp.zeros((1, n_dirs), f32)

    def times(a, b):
        return a[0] * b[0] - a[1] * b[1], a[0] * b[1] + a[1] * b[0]

    coef = [None] * n_strip
    run = (one, zero)
    for q in reversed(range(n_strip)):
        t = (shf_ref[q, 0:1, :], shf_ref[q, 1:2, :])
        coef[q] = tuple(jnp.where(q < strip, part, 0.0) for part in run)
        run = times((jnp.where(q <= strip, t[0], 1.0), jnp.where(q <= strip, t[1], 0.0)), run)
    run = (one, zero)
    for q in range(n_strip):
        t = (shf_ref[q, 0:1, :], -shf_ref[q, 1:2, :])
        coef[q] = tuple(a + jnp.where(q > strip, part, 0.0) for a, part in zip(coef[q], run))
        run = times((jnp.where(q >= strip, t[0], 1.0), jnp.where(q >= strip, t[1], 0.0)), run)
    stacked = jnp.concatenate([c[0] for c in coef] + [c[1] for c in coef], axis=0)
    coef_ref[...] = stacked.T
    here = coef_ref[pl.ds(pl.multiple_of(sub * quarter, quarter), quarter), :]

    cen_col = cen_ref[...].reshape(all_box, 128)
    cen_row = cen_col.T
    col_x, col_y = cen_col[:, 0:1], cen_col[:, 1:2]
    row_x, row_y = cen_row[0:1, :], cen_row[1:2, :]
    step = 2.0 * math.pi / n_dirs
    k_col = lax.broadcasted_iota(jnp.int32, (quarter, all_box), 0) + sub * quarter
    angle = k_col.astype(f32) * step
    mid_x = (strip.astype(f32) + 0.5) * rows_x
    mid_y = 0.5 * rows_y * n_sub
    psi = wave_number * ((row_x - mid_x) * jnp.cos(angle) + (row_y - mid_y) * jnp.sin(angle))
    psi_re, psi_im = jnp.cos(psi), jnp.sin(psi)

    fold = 128 // all_box
    dx = col_x - jnp.concatenate([row_x] * fold, axis=1)
    dy = col_y - jnp.concatenate([row_y] * fold, axis=1)
    rho = jnp.sqrt(dx * dx + dy * dy)
    lane = lax.broadcasted_iota(jnp.int32, (all_box, 128), 1)
    target = lax.broadcasted_iota(jnp.int32, (all_box, 128), 0)
    amplitude = jnp.where(lane % all_box != target, 1.0 / (1.0 + rho), 0.0)
    lane_k = lax.broadcasted_iota(jnp.int32, (1, 128), 1) // all_box

    def weights(g, carry):
        turn = (lane_k + g * fold + sub * quarter).astype(f32) * step
        arg = wave_number * (rho + jnp.cos(turn) * dx + jnp.sin(turn) * dy)
        w_re = (amplitude * jnp.cos(arg)).astype(bf16).astype(f32)
        w_im = (amplitude * jnp.sin(arg)).astype(bf16).astype(f32)
        for i in range(fold):
            part = slice(i * all_box, (i + 1) * all_box)
            a, b = w_re[:, part], w_im[:, part]
            w_ref[g * fold + i] = jnp.concatenate(
                [jnp.concatenate([a, -b], axis=1), jnp.concatenate([b, a], axis=1)], axis=0
            ).astype(bf16)
        return carry

    lax.fori_loop(0, quarter // fold, weights, 0)

    def source(d):
        return lax.rem(sub + n_sub - d, n_sub)

    for d in range(n_sub):
        if d:
            a2a_copy(d).wait_recv()
        base = source(d)
        for b in range(n_box):
            for c in range(2):
                block = box_ref[sub, b, c] if d == 0 else in_ref[d, b, c]
                at = (c * all_box + base * n_box + b) * quarter
                wide_ref[pl.ds(pl.multiple_of(at, quarter), quarter), :] = block.astype(f32)

    total_re = jnp.zeros((quarter, n_sides), f32)
    total_im = jnp.zeros((quarter, n_sides), f32)
    for b in range(all_box):
        p_re, p_im = psi_re[:, b : b + 1], psi_im[:, b : b + 1]
        v_re = wide_ref[b * quarter : (b + 1) * quarter, :]
        v_im = wide_ref[(all_box + b) * quarter : (all_box + b + 1) * quarter, :]
        total_re += p_re * v_re - p_im * v_im
        total_im += p_im * v_re + p_re * v_im
    exp_ref[strip, 0] = (strip_weight * total_re).astype(bf16)
    exp_ref[strip, 1] = (strip_weight * total_im).astype(bf16)

    def send_exp(d, carry):
        strip_copy(exp_ref, exp_send, exp_recv, d, strip).start()
        return carry

    lax.fori_loop(1, n_strip, send_exp, 0)

    def interact(k, carry):
        rhs = wide_ref[pl.ds(k, 2 * all_box, stride=quarter), :].astype(bf16)
        inc_ref[pl.ds(k, 2 * all_box, stride=quarter), :] = jnp.dot(
            w_ref[k], rhs, preferred_element_type=f32
        )
        return carry

    lax.fori_loop(0, quarter, interact, 0)

    def wait_exp(d, carry):
        src = lax.rem(strip + n_strip - d, n_strip)
        strip_copy(exp_ref, exp_send, exp_recv, d, src).wait_recv()
        return carry

    lax.fori_loop(1, n_strip, wait_exp, 0)
    field_re = jnp.zeros((quarter, n_sides), f32)
    field_im = jnp.zeros((quarter, n_sides), f32)
    for q in range(n_strip):
        c_re, c_im = here[:, q : q + 1], here[:, n_strip + q : n_strip + q + 1]
        v_re, v_im = exp_ref[q, 0].astype(f32), exp_ref[q, 1].astype(f32)
        field_re += c_re * v_re - c_im * v_im
        field_im += c_re * v_im + c_im * v_re
    for b in range(all_box):
        p_re, p_im = psi_re[:, b : b + 1], psi_im[:, b : b + 1]
        v_re = inc_ref[b * quarter : (b + 1) * quarter, :]
        v_im = inc_ref[(all_box + b) * quarter : (all_box + b + 1) * quarter, :]
        send_ref[b // n_box, b % n_box, 0] = (v_re + p_re * field_re + p_im * field_im).astype(bf16)
        send_ref[b // n_box, b % n_box, 1] = (v_im + p_re * field_im - p_im * field_re).astype(bf16)

    def back_copy(d, at):
        return pltpu.make_async_remote_copy(
            src_ref=send_ref.at[sub_peer(d)], dst_ref=lf_ref.at[at],
            send_sem=back_send.at[d], recv_sem=back_recv.at[d],
            device_id=(strip, sub_peer(d)), device_id_type=MESH,
        )

    for d in range(1, n_sub):
        back_copy(d, sub).start()
    lf_ref[sub] = send_ref[sub]

    for n in range(len(offsets)):
        halo_copy(n).wait_recv()
    near_part(located_ref, nb_ref, flat_pad, near_ref, a_ref, x_ref)

    for d in range(1, n_sub):
        back_copy(d, source(d)).wait_recv()
    far_part(perm_ref, slot_ref, lf_ref, dis_ref, cos_ref, sin_ref, near_ref, out_ref, e_ref, far_ref)

    for d in range(1, n_sub):
        cen_copy(d).wait_send()
        a2a_copy(d).wait_send()
        back_copy(d, sub).wait_send()

    def drain(d, carry):
        strip_copy(shf_ref, shf_send, shf_recv, d, strip).wait_send()
        strip_copy(exp_ref, exp_send, exp_recv, d, strip).wait_send()
        return carry

    lax.fori_loop(1, n_strip, drain, 0)
    for n in range(len(offsets)):
        halo_copy(n).wait_send()


def per_device(
    currents,
    near_blocks,
    near_index,
    box_of_patch,
    box_centre,
    patch_angle,
    aggregation,
    disaggregation,
    strip_shift,
):
    rows_x, rows_y, n_units, n_sides = currents.shape
    n_dirs = patch_angle.shape[2]
    n_slots = near_index.shape[2]
    n_patch = rows_x * rows_y
    box_dev = box_centre.shape[0]
    n_sub = lax.axis_size("sub")
    n_strip = lax.axis_size("strip")
    strip_pos = lax.axis_index("strip")
    sub_pos = lax.axis_index("sub")
    ny_total = rows_y * n_sub
    quarter = n_dirs // n_sub
    all_box = box_dev * n_sub
    wanted = near_index.reshape(n_patch * n_slots)
    located = (wanted // ny_total - strip_pos * rows_x + 1) * (rows_y + 2) + (
        wanted % ny_total - sub_pos * rows_y + 1
    )
    located = jnp.where(wanted >= 0, located, (rows_x + 2) * (rows_y + 2))
    ids = jnp.arange(n_patch, dtype=jnp.int32)
    key = box_of_patch.reshape(n_patch) * n_patch + ids
    slot = jnp.sum((key[None, :] < key[:, None]).astype(jnp.int32), axis=1)
    perm = jnp.sum(jnp.where(slot[None, :] == ids[:, None], ids[None, :], 0), axis=1)
    smem = pl.BlockSpec(memory_space=pltpu.SMEM)
    vmem = pl.BlockSpec(memory_space=pltpu.VMEM)
    dma = pltpu.SemaphoreType.DMA
    scratch = [
        pltpu.VMEM((rows_x + 3, rows_y + 2, n_units, n_sides), bf16),
        pltpu.VMEM((n_sub, box_dev, 2, quarter, n_sides), bf16),
        pltpu.VMEM((n_patch, n_dirs), f32),
        pltpu.VMEM((n_patch, n_dirs), f32),
        pltpu.VMEM((n_slots * n_units, n_sides), bf16),
        pltpu.VMEM((n_patch // box_dev * n_units, 2 * n_dirs), bf16),
        pltpu.VMEM((n_patch, n_units, n_sides), f32),
        pltpu.VMEM((128, 128), f32),
        pltpu.VMEM((n_patch, n_units, n_sides), f32),
        pltpu.VMEM((n_sub, box_dev, 2, quarter, n_sides), bf16),
        pltpu.VMEM((n_sub, box_dev, 128), f32),
        pltpu.VMEM((n_strip, 8, n_dirs), f32),
        pltpu.VMEM((n_sub, box_dev, 2, quarter, n_sides), bf16),
        pltpu.VMEM((2 * all_box * quarter, n_sides), f32),
        pltpu.VMEM((quarter, 2 * all_box, 2 * all_box), bf16),
        pltpu.VMEM((2 * all_box * quarter, n_sides), f32),
        pltpu.VMEM((n_strip, 2, quarter, n_sides), bf16),
        pltpu.VMEM((n_dirs, 2 * n_strip), f32),
        pltpu.VMEM((n_sub, box_dev, 2, quarter, n_sides), bf16),
        dma((8,)), dma((8,)),
        dma((n_sub,)), dma((n_sub,)),
        dma((n_strip,)), dma((n_strip,)),
        dma((n_sub,)), dma((n_sub,)),
        dma((n_strip,)), dma((n_strip,)),
        dma((n_sub,)), dma((n_sub,)),
    ]
    result = pl.pallas_call(
        functools.partial(fused, n_strip, n_sub),
        out_shape=jax.ShapeDtypeStruct((n_patch, n_units, n_sides), bf16),
        in_specs=[smem] * 3 + [vmem] * 7,
        out_specs=vmem,
        scratch_shapes=scratch,
        compiler_params=pltpu.CompilerParams(
            collective_id=0, has_side_effects=True, vmem_limit_bytes=48 * 1024 * 1024
        ),
    )(
        perm,
        slot,
        located,
        currents,
        near_blocks.reshape(n_patch, n_slots, n_units * n_units),
        patch_angle.reshape(n_patch, n_dirs),
        jnp.swapaxes(aggregation, 1, 2).astype(f32),
        jnp.swapaxes(disaggregation, 1, 2).astype(f32),
        box_centre,
        strip_shift,
    )
    return result.reshape(rows_x, rows_y, n_units, n_sides)


def solution(mesh):
    in_specs = (
        P("strip", "sub", None, None),
        P("strip", "sub", None, None),
        P("strip", "sub", None),
        P("strip", "sub"),
        P(("strip", "sub"), None),
        P("strip", "sub", None),
        P(),
        P(),
        P("strip", None, None),
    )
    out_specs = P("strip", "sub", None, None)
    return jax.shard_map(
        per_device, mesh=mesh, in_specs=in_specs, out_specs=out_specs, check_vma=False
    )
```

```python
import functools
import math

import jax
import jax.numpy as jnp
from jax import lax
from jax.experimental import pallas as pl
from jax.experimental.pallas import tpu as pltpu
from jax.sharding import PartitionSpec as P

wave_number = 1.5
strip_weight = 0.03
NSPLIT = 1
LATER = 2
MESH = pl.DeviceIdType.MESH
f32 = jnp.float32
bf16 = jnp.bfloat16


def gather_boxes(perm_ref, cur_ref, angle_ref, agg_ref, box_ref, cos_ref, sin_ref):
    n_sub, n_box, _, quarter, _ = box_ref.shape
    n_patch, n_dirs = angle_ref.shape
    n_units = cur_ref.shape[1]
    per_box = n_patch // n_box
    cos_ref[...] = jnp.cos(angle_ref[...])
    sin_ref[...] = jnp.sin(angle_ref[...])

    agg_re, agg_im = agg_ref[0].astype(f32), agg_ref[1].astype(f32)

    def one_box(b):
        rows_e, rows_x = [], []
        for i in range(per_box):
            p = perm_ref[b * per_box + i]
            rows_x.append(cur_ref[p])
            c = cos_ref[pl.ds(p, 1), :]
            s = sin_ref[pl.ds(p, 1), :]
            rows_e.append(
                jnp.concatenate([c * agg_re - s * agg_im, s * agg_re + c * agg_im], axis=1).astype(bf16)
            )
        values = lax.dot_general(
            jnp.concatenate(rows_e, axis=0),
            jnp.concatenate(rows_x, axis=0),
            (((0,), (0,)), ((), ())),
            preferred_element_type=f32,
        ).astype(bf16)
        for c in range(2):
            for q in range(n_sub):
                at = c * n_dirs + q * quarter
                box_ref[q, b, c] = values[at : at + quarter]

    def two_boxes(h, carry):
        one_box(2 * h)
        one_box(2 * h + 1)
        return carry

    lax.fori_loop(0, n_box // 2, two_boxes, 0)


def near_part(first, last, located_ref, nb_ref, pad_ref, near_ref, a_ref):
    _, n_slots, rows_y, _ = nb_ref.shape
    n_units, n_sides = near_ref.shape[1:]
    lanes = lax.broadcasted_iota(jnp.int32, (8, 128), 1) // 32

    def pick(parts):
        out = parts[0]
        for i in range(1, 4):
            out = jnp.where(lanes == i, parts[i], out)
        return out

    def one_patch(x, y):
        p = x * rows_y + y
        found = [pad_ref[located_ref[j, x, y]] for j in range(n_slots)]
        flat = [a_ref[pl.ds(j * 8 * rows_y + y, 8, stride=rows_y), :] for j in range(n_slots)]
        lhs = []
        for g in range(2):
            group = flat[g * 4 : g * 4 + 4]
            rolled = []
            for d in range(4):
                mixed = pick([group[(u + d) % 4] for u in range(4)])
                rolled.append(mixed if d == 0 else pltpu.roll(mixed, 32 * d, 1))
            lhs.append(
                jnp.concatenate([pick([rolled[(j - u) % 4] for j in range(4)]) for u in range(4)], axis=0)
            )
        tail = jnp.concatenate(
            [flat[8]] + [pltpu.roll(flat[8], 128 - 32 * u, 1) for u in range(1, 4)], axis=0
        )
        total = jnp.dot(
            jnp.concatenate(lhs, axis=1).astype(bf16),
            jnp.concatenate(found[0:8], axis=0),
            preferred_element_type=f32,
        )
        total += jnp.dot(tail[:, 0:n_units].astype(bf16), found[8], preferred_element_type=f32)
        for u in range(4):
            near_ref[p, pl.ds(u, 8, stride=4), :] = total[u * 8 : u * 8 + 8]

    def one_row(x, carry):
        for j in range(n_slots):
            for q in range(8):
                at = (j * 8 + q) * rows_y
                a_ref[at : at + rows_y, :] = nb_ref[x, j, :, q * 128 : (q + 1) * 128].astype(f32)

        def some(g, inner):
            for i in range(4):
                one_patch(x, g * 4 + i)
            return inner

        return lax.fori_loop(0, rows_y // 4, some, carry)

    lax.fori_loop(first, last, one_row, 0)


def far_part(perm_ref, slot_ref, lf_ref, dis_ref, cos_ref, sin_ref, near_ref, out_ref, far_ref):
    n_sub, n_box, _, quarter, n_sides = lf_ref.shape
    n_patch, n_dirs = cos_ref.shape
    n_units = near_ref.shape[1]
    per_box = n_patch // n_box

    dis_re, dis_im = dis_ref[0].astype(f32), dis_ref[1].astype(f32)

    def one_box(b):
        rows_d = []
        for i in range(per_box):
            p = perm_ref[b * per_box + i]
            c = cos_ref[pl.ds(p, 1), :]
            s = sin_ref[pl.ds(p, 1), :]
            rows_d.append(
                jnp.concatenate([c * dis_re - s * dis_im, s * dis_re + c * dis_im], axis=1).astype(bf16)
            )
        field = jnp.concatenate([lf_ref[q, b, c] for c in range(2) for q in range(n_sub)], axis=0)
        far = jnp.dot(jnp.concatenate(rows_d, axis=0), field, preferred_element_type=f32)
        for i in range(per_box):
            far_ref[b * per_box + i] = far[i * n_units : (i + 1) * n_units]

    def two_boxes(h, carry):
        one_box(2 * h)
        one_box(2 * h + 1)
        return carry

    lax.fori_loop(0, n_box // 2, two_boxes, 0)

    def some_patches(h, carry):
        for i in range(8):
            p = h * 8 + i
            out_ref[p] = (near_ref[p] + far_ref[slot_ref[p]]).astype(bf16)
        return carry

    lax.fori_loop(0, n_patch // 8, some_patches, 0)


def fused(
    n_strip, n_sub,
    perm_ref, slot_ref, index_ref, cur_ref, nb_ref, angle_ref, agg_ref, dis_ref, centre_ref, shift_ref,
    out_ref,
    pad_ref, box_ref, cos_ref, sin_ref, near_ref, a_ref, far_ref, lf_ref,
    cen_ref, shf_ref, in_ref, wide_ref, w_ref, inc_ref, exp_ref, coef_ref, send_ref, place_ref, located_ref, place_sem,
    halo_send, halo_recv, cen_send, cen_recv, shf_send, shf_recv, a2a_send, a2a_recv,
    exp_send, exp_recv, back_send, back_recv,
):
    strip = lax.axis_index("strip")
    sub = lax.axis_index("sub")
    rows_x, rows_y = cur_ref.shape[0], cur_ref.shape[1]
    n_units, n_sides = cur_ref.shape[2], cur_ref.shape[3]
    n_patch = rows_x * rows_y
    n_dirs = angle_ref.shape[1]
    quarter = n_dirs // n_sub
    n_box = centre_ref.shape[1]
    all_box = n_box * n_sub
    wide_y = rows_y + 2

    def sub_peer(d):
        return lax.rem(sub + d, n_sub)

    def strip_peer(d):
        return lax.rem(strip + d, n_strip)

    offsets = [(dx, dy) for dx in (-1, 0, 1) for dy in (-1, 0, 1) if dx or dy]

    barrier = pltpu.get_barrier_semaphore()
    for dx in (-1, 1):
        for dy in (-1, 1):
            pl.semaphore_signal(
                barrier, inc=1, device_id=(strip_peer(dx + n_strip), sub_peer(dy + n_sub)), device_id_type=MESH
            )
    for d in range(1, n_sub):
        pl.semaphore_signal(barrier, inc=1, device_id=(strip, sub_peer(d)), device_id_type=MESH)

    def greet(d, carry):
        pl.semaphore_signal(barrier, inc=1, device_id=(strip_peer(d), sub), device_id_type=MESH)
        return carry

    lax.fori_loop(1, n_strip, greet, 0)

    cen_ref[sub] = jnp.zeros((8, 128), f32)
    cen_ref[sub, 0:2, 0:n_box] = centre_ref[...]
    wanted = index_ref[...]
    ny_total = rows_y * n_sub
    row = wanted // ny_total
    place = (row - strip * rows_x + 1) * wide_y + (wanted - row * ny_total - sub * rows_y + 1)
    empty = (rows_x + 2) * wide_y
    place = jnp.minimum(jnp.maximum(place, 0), empty)
    place_ref[...] = jnp.where(wanted >= 0, place, empty)
    placing = pltpu.make_async_copy(place_ref, located_ref, place_sem)
    placing.start()
    shf_ref[strip] = jnp.zeros((8, n_dirs), f32)
    shf_ref[strip, 0:2, :] = shift_ref[0]
    pl.semaphore_wait(barrier, 4 + n_sub - 1 + n_strip - 1)

    def cen_copy(d):
        return pltpu.make_async_remote_copy(
            src_ref=cen_ref.at[sub], dst_ref=cen_ref.at[sub],
            send_sem=cen_send.at[d], recv_sem=cen_recv.at[d],
            device_id=(strip, sub_peer(d)), device_id_type=MESH,
        )

    def cen_wait(d):
        src = lax.rem(sub + n_sub - d, n_sub)
        return pltpu.make_async_remote_copy(
            src_ref=cen_ref.at[src], dst_ref=cen_ref.at[src],
            send_sem=cen_send.at[d], recv_sem=cen_recv.at[d],
            device_id=(strip, sub_peer(d)), device_id_type=MESH,
        )

    def strip_copy(buf, send, recv, d, at):
        return pltpu.make_async_remote_copy(
            src_ref=buf.at[at], dst_ref=buf.at[at],
            send_sem=send.at[d], recv_sem=recv.at[d],
            device_id=(strip_peer(d), sub), device_id_type=MESH,
        )

    def halo_copy(n):
        dx, dy = offsets[n]
        src_x = {-1: slice(0, 1), 0: slice(0, rows_x), 1: slice(rows_x - 1, rows_x)}[dx]
        src_y = {-1: slice(0, 1), 0: slice(0, rows_y), 1: slice(rows_y - 1, rows_y)}[dy]
        dst_x = {-1: slice(rows_x + 1, rows_x + 2), 0: slice(1, rows_x + 1), 1: slice(0, 1)}[dx]
        dst_y = {-1: slice(rows_y + 1, rows_y + 2), 0: slice(1, rows_y + 1), 1: slice(0, 1)}[dy]
        return pltpu.make_async_remote_copy(
            src_ref=cur_ref.at[src_x, src_y], dst_ref=pad_ref.at[dst_x, dst_y],
            send_sem=halo_send.at[n], recv_sem=halo_recv.at[n],
            device_id=(strip_peer(dx + n_strip), sub_peer(dy + n_sub)), device_id_type=MESH,
        )

    for d in range(1, n_sub):
        cen_copy(d).start()

    def send_shift(d, carry):
        strip_copy(shf_ref, shf_send, shf_recv, d, strip).start()
        return carry

    lax.fori_loop(1, n_strip, send_shift, 0)
    for n in range(len(offsets)):
        halo_copy(n).start()

    flat_cur = cur_ref.reshape(n_patch, n_units, n_sides)
    flat_pad = pad_ref.reshape((rows_x + 3) * wide_y, n_units, n_sides)

    gather_boxes(perm_ref, flat_cur, angle_ref, agg_ref, box_ref, cos_ref, sin_ref)

    def a2a_copy(d):
        return pltpu.make_async_remote_copy(
            src_ref=box_ref.at[sub_peer(d)], dst_ref=in_ref.at[d],
            send_sem=a2a_send.at[d], recv_sem=a2a_recv.at[d],
            device_id=(strip, sub_peer(d)), device_id_type=MESH,
        )

    for d in range(1, n_sub):
        a2a_copy(d).start()

    for x in range(rows_x):
        pad_ref[x + 1, 1 : rows_y + 1] = cur_ref[x]
    pad_ref[rows_x + 2, 0] = jnp.zeros((n_units, n_sides), bf16)

    def wait_shift(d, carry):
        src = lax.rem(strip + n_strip - d, n_strip)
        strip_copy(shf_ref, shf_send, shf_recv, d, src).wait_recv()
        return carry

    lax.fori_loop(1, n_strip, wait_shift, 0)
    for d in range(1, n_sub):
        cen_wait(d).wait_recv()
    one = jnp.ones((1, n_dirs), f32)
    zero = jnp.zeros((1, n_dirs), f32)

    def times(a, b):
        return a[0] * b[0] - a[1] * b[1], a[0] * b[1] + a[1] * b[0]

    coef = [None] * n_strip
    run = (one, zero)
    for q in reversed(range(n_strip)):
        t = (shf_ref[q, 0:1, :], shf_ref[q, 1:2, :])
        coef[q] = tuple(jnp.where(q < strip, part, 0.0) for part in run)
        run = times((jnp.where(q <= strip, t[0], 1.0), jnp.where(q <= strip, t[1], 0.0)), run)
    run = (one, zero)
    for q in range(n_strip):
        t = (shf_ref[q, 0:1, :], -shf_ref[q, 1:2, :])
        coef[q] = tuple(a + jnp.where(q > strip, part, 0.0) for a, part in zip(coef[q], run))
        run = times((jnp.where(q >= strip, t[0], 1.0), jnp.where(q >= strip, t[1], 0.0)), run)
    stacked = jnp.concatenate([c[0] for c in coef] + [c[1] for c in coef], axis=0)
    coef_ref[...] = stacked.T
    here = coef_ref[pl.ds(pl.multiple_of(sub * quarter, quarter), quarter), :]

    cen_row = jnp.concatenate([cen_ref[i, :, 0:n_box] for i in range(n_sub)], axis=1)
    cen_col = jnp.concatenate([cen_ref[i].T[0:n_box, :] for i in range(n_sub)], axis=0)
    col_x, col_y = cen_col[:, 0:1], cen_col[:, 1:2]
    row_x, row_y = cen_row[0:1, :], cen_row[1:2, :]
    step = 2.0 * math.pi / n_dirs
    k_col = lax.broadcasted_iota(jnp.int32, (quarter, all_box), 0) + sub * quarter
    angle = k_col.astype(f32) * step
    mid_x = (strip.astype(f32) + 0.5) * rows_x
    mid_y = 0.5 * rows_y * n_sub
    psi = wave_number * ((row_x - mid_x) * jnp.cos(angle) + (row_y - mid_y) * jnp.sin(angle))
    psi_re, psi_im = jnp.cos(psi), jnp.sin(psi)

    fold = 128 // all_box
    dx = col_x - jnp.concatenate([row_x] * fold, axis=1)
    dy = col_y - jnp.concatenate([row_y] * fold, axis=1)
    rho = jnp.sqrt(dx * dx + dy * dy)
    lane = lax.broadcasted_iota(jnp.int32, (all_box, 128), 1)
    target = lax.broadcasted_iota(jnp.int32, (all_box, 128), 0)
    amplitude = jnp.where(lane % all_box != target, 1.0 / (1.0 + rho), 0.0)
    lane_k = lax.broadcasted_iota(jnp.int32, (1, 128), 1) // all_box

    def weights(g, carry):
        turn = (lane_k + g * fold + sub * quarter).astype(f32) * step
        arg = wave_number * (rho + jnp.cos(turn) * dx + jnp.sin(turn) * dy)
        w_re = (amplitude * jnp.cos(arg)).astype(bf16).astype(f32)
        w_im = (amplitude * jnp.sin(arg)).astype(bf16).astype(f32)
        for i in range(fold):
            part = slice(i * all_box, (i + 1) * all_box)
            a, b = w_re[:, part], w_im[:, part]
            w_ref[g * fold + i] = jnp.concatenate(
                [jnp.concatenate([a, -b], axis=1), jnp.concatenate([b, a], axis=1)], axis=0
            ).astype(bf16)
        return carry

    lax.fori_loop(0, quarter // fold, weights, 0)

    placing.wait()
    for n in range(len(offsets)):
        halo_copy(n).wait_recv()
    split = NSPLIT * rows_x // 4
    later = LATER * rows_x // 4
    near_part(0, split, located_ref, nb_ref, flat_pad, near_ref, a_ref)

    def source(d):
        return lax.rem(sub + n_sub - d, n_sub)

    for d in range(n_sub):
        if d:
            a2a_copy(d).wait_recv()
        base = source(d)
        for b in range(n_box):
            for c in range(2):
                block = box_ref[sub, b, c] if d == 0 else in_ref[d, b, c]
                at = (c * all_box + base * n_box + b) * quarter
                wide_ref[pl.ds(pl.multiple_of(at, quarter), quarter), :] = block.astype(f32)

    total_re = jnp.zeros((quarter, n_sides), f32)
    total_im = jnp.zeros((quarter, n_sides), f32)
    for b in range(all_box):
        p_re, p_im = psi_re[:, b : b + 1], psi_im[:, b : b + 1]
        v_re = wide_ref[b * quarter : (b + 1) * quarter, :]
        v_im = wide_ref[(all_box + b) * quarter : (all_box + b + 1) * quarter, :]
        total_re += p_re * v_re - p_im * v_im
        total_im += p_im * v_re + p_re * v_im
    exp_ref[strip, 0] = (strip_weight * total_re).astype(bf16)
    exp_ref[strip, 1] = (strip_weight * total_im).astype(bf16)

    def send_exp(d, carry):
        strip_copy(exp_ref, exp_send, exp_recv, d, strip).start()
        return carry

    lax.fori_loop(1, n_strip, send_exp, 0)

    def interact(g, carry):
        ks = [g * 8 + i for i in range(8)]
        rhs = [wide_ref[pl.ds(k, 2 * all_box, stride=quarter), :].astype(bf16) for k in ks]
        out = [jnp.dot(w_ref[k], v, preferred_element_type=f32) for k, v in zip(ks, rhs)]
        for k, v in zip(ks, out):
            inc_ref[pl.ds(k, 2 * all_box, stride=quarter), :] = v
        return carry

    lax.fori_loop(0, quarter // 8, interact, 0)

    def wait_exp(d, carry):
        src = lax.rem(strip + n_strip - d, n_strip)
        strip_copy(exp_ref, exp_send, exp_recv, d, src).wait_recv()
        return carry

    near_part(split, later, located_ref, nb_ref, flat_pad, near_ref, a_ref)
    lax.fori_loop(1, n_strip, wait_exp, 0)
    field_re = jnp.zeros((quarter, n_sides), f32)
    field_im = jnp.zeros((quarter, n_sides), f32)
    for q in range(n_strip):
        c_re, c_im = here[:, q : q + 1], here[:, n_strip + q : n_strip + q + 1]
        v_re, v_im = exp_ref[q, 0].astype(f32), exp_ref[q, 1].astype(f32)
        field_re += c_re * v_re - c_im * v_im
        field_im += c_re * v_im + c_im * v_re
    def back_copy(d, at, to):
        return pltpu.make_async_remote_copy(
            src_ref=send_ref.at[to], dst_ref=lf_ref.at[at],
            send_sem=back_send.at[d], recv_sem=back_recv.at[d],
            device_id=(strip, to), device_id_type=MESH,
        )

    for b in range(all_box):
        p_re, p_im = psi_re[:, b : b + 1], psi_im[:, b : b + 1]
        v_re = inc_ref[b * quarter : (b + 1) * quarter, :]
        v_im = inc_ref[(all_box + b) * quarter : (all_box + b + 1) * quarter, :]
        send_ref[b // n_box, b % n_box, 0] = (v_re + p_re * field_re + p_im * field_im).astype(bf16)
        send_ref[b // n_box, b % n_box, 1] = (v_im + p_re * field_im - p_im * field_re).astype(bf16)
        if b % n_box == n_box - 1:
            to = b // n_box

            @pl.when(to != sub)
            def _(to=to):
                back_copy(lax.rem(to - sub + n_sub, n_sub), sub, to).start()


    lf_ref[sub] = send_ref[sub]

    near_part(later, rows_x, located_ref, nb_ref, flat_pad, near_ref, a_ref)

    for d in range(1, n_sub):
        back_copy(d, source(d), sub_peer(d)).wait_recv()
    far_part(perm_ref, slot_ref, lf_ref, dis_ref, cos_ref, sin_ref, near_ref, out_ref, far_ref)

    for d in range(1, n_sub):
        cen_copy(d).wait_send()
        a2a_copy(d).wait_send()
        back_copy(d, sub, sub_peer(d)).wait_send()

    def drain(d, carry):
        strip_copy(shf_ref, shf_send, shf_recv, d, strip).wait_send()
        strip_copy(exp_ref, exp_send, exp_recv, d, strip).wait_send()
        return carry

    lax.fori_loop(1, n_strip, drain, 0)
    for n in range(len(offsets)):
        halo_copy(n).wait_send()


def per_device(
    currents,
    near_blocks,
    near_index,
    box_of_patch,
    box_centre,
    patch_angle,
    aggregation,
    disaggregation,
    strip_shift,
):
    rows_x, rows_y, n_units, n_sides = currents.shape
    n_dirs = patch_angle.shape[2]
    n_slots = near_index.shape[2]
    n_patch = rows_x * rows_y
    box_dev = box_centre.shape[0]
    n_sub = lax.axis_size("sub")
    n_strip = lax.axis_size("strip")
    quarter = n_dirs // n_sub
    all_box = box_dev * n_sub
    ids = jnp.arange(n_patch, dtype=jnp.int32)
    key = box_of_patch.reshape(n_patch) * n_patch + ids
    slot = jnp.sum((key[None, :] < key[:, None]).astype(jnp.int32), axis=1)
    perm = jnp.sum(jnp.where(slot[None, :] == ids[:, None], ids[None, :], 0), axis=1)
    smem = pl.BlockSpec(memory_space=pltpu.SMEM)
    vmem = pl.BlockSpec(memory_space=pltpu.VMEM)
    dma = pltpu.SemaphoreType.DMA
    scratch = [
        pltpu.VMEM((rows_x + 3, rows_y + 2, n_units, n_sides), bf16),
        pltpu.VMEM((n_sub, box_dev, 2, quarter, n_sides), bf16),
        pltpu.VMEM((n_patch, n_dirs), f32),
        pltpu.VMEM((n_patch, n_dirs), f32),
        pltpu.VMEM((n_patch, n_units, n_sides), f32),
        pltpu.VMEM((n_slots * 8 * rows_y, 128), f32),
        pltpu.VMEM((n_patch, n_units, n_sides), f32),
        pltpu.VMEM((n_sub, box_dev, 2, quarter, n_sides), bf16),
        pltpu.VMEM((n_sub, 8, 128), f32),
        pltpu.VMEM((n_strip, 8, n_dirs), f32),
        pltpu.VMEM((n_sub, box_dev, 2, quarter, n_sides), bf16),
        pltpu.VMEM((2 * all_box * quarter, n_sides), f32),
        pltpu.VMEM((quarter, 2 * all_box, 2 * all_box), bf16),
        pltpu.VMEM((2 * all_box * quarter, n_sides), f32),
        pltpu.VMEM((n_strip, 2, quarter, n_sides), bf16),
        pltpu.VMEM((n_dirs, 2 * n_strip), f32),
        pltpu.VMEM((n_sub, box_dev, 2, quarter, n_sides), bf16),
        pltpu.VMEM((n_slots, rows_x, rows_y), jnp.int32),
        pltpu.SMEM((n_slots, rows_x, rows_y), jnp.int32),
        dma(()),
        dma((8,)), dma((8,)),
        dma((n_sub,)), dma((n_sub,)),
        dma((n_strip,)), dma((n_strip,)),
        dma((n_sub,)), dma((n_sub,)),
        dma((n_strip,)), dma((n_strip,)),
        dma((n_sub,)), dma((n_sub,)),
    ]
    result = pl.pallas_call(
        functools.partial(fused, n_strip, n_sub),
        out_shape=jax.ShapeDtypeStruct((n_patch, n_units, n_sides), bf16),
        in_specs=[smem] * 2 + [vmem] * 8,
        out_specs=vmem,
        scratch_shapes=scratch,
        compiler_params=pltpu.CompilerParams(
            collective_id=0, has_side_effects=True, vmem_limit_bytes=48 * 1024 * 1024
        ),
    )(
        perm,
        slot,
        jnp.transpose(near_index, (2, 0, 1)),
        currents,
        jnp.transpose(near_blocks, (0, 2, 1, 3)),
        patch_angle.reshape(n_patch, n_dirs),
        jnp.swapaxes(aggregation, 1, 2),
        jnp.swapaxes(disaggregation, 1, 2),
        box_centre.T,
        strip_shift,
    )
    return result.reshape(rows_x, rows_y, n_units, n_sides)


def solution(mesh):
    in_specs = (
        P("strip", "sub", None, None),
        P("strip", "sub", None, None),
        P("strip", "sub", None),
        P("strip", "sub"),
        P(("strip", "sub"), None),
        P("strip", "sub", None),
        P(),
        P(),
        P("strip", None, None),
    )
    out_specs = P("strip", "sub", None, None)
    return jax.shard_map(
        per_device, mesh=mesh, in_specs=in_specs, out_specs=out_specs, check_vma=False
    )
```

```python
import functools
import math

import jax
import jax.numpy as jnp
from jax import lax
from jax.experimental import pallas as pl
from jax.experimental.pallas import tpu as pltpu
from jax.sharding import PartitionSpec as P

wave_number = 1.5
strip_weight = 0.03
NSPLIT = 1
LATER = 2
MESH = pl.DeviceIdType.MESH
f32 = jnp.float32
bf16 = jnp.bfloat16


def gather_boxes(perm_ref, cur_ref, angle_ref, agg_ref, box_ref, cos_ref, sin_ref):
    n_sub, n_box, _, quarter, _ = box_ref.shape
    n_patch, n_dirs = angle_ref.shape
    n_units = cur_ref.shape[1]
    per_box = n_patch // n_box
    cos_ref[...] = jnp.cos(angle_ref[...])
    sin_ref[...] = jnp.sin(angle_ref[...])

    agg_re, agg_im = agg_ref[0].astype(f32), agg_ref[1].astype(f32)

    def one_box(b):
        rows_e, rows_x = [], []
        for i in range(per_box):
            p = perm_ref[b * per_box + i]
            rows_x.append(cur_ref[p])
            c = cos_ref[pl.ds(p, 1), :]
            s = sin_ref[pl.ds(p, 1), :]
            rows_e.append(
                jnp.concatenate([c * agg_re - s * agg_im, s * agg_re + c * agg_im], axis=1).astype(bf16)
            )
        values = lax.dot_general(
            jnp.concatenate(rows_e, axis=0),
            jnp.concatenate(rows_x, axis=0),
            (((0,), (0,)), ((), ())),
            preferred_element_type=f32,
        ).astype(bf16)
        for c in range(2):
            for q in range(n_sub):
                at = c * n_dirs + q * quarter
                box_ref[q, b, c] = values[at : at + quarter]

    def two_boxes(h, carry):
        one_box(2 * h)
        one_box(2 * h + 1)
        return carry

    lax.fori_loop(0, n_box // 2, two_boxes, 0)


def near_part(first, last, located_ref, nb_ref, pad_ref, near_ref, a_ref):
    _, n_slots, rows_y, _ = nb_ref.shape
    n_units, n_sides = near_ref.shape[1:]
    lanes = lax.broadcasted_iota(jnp.int32, (8, 128), 1) // 32

    def pick(parts):
        out = parts[0]
        for i in range(1, 4):
            out = jnp.where(lanes == i, parts[i], out)
        return out

    def one_patch(x, y):
        p = x * rows_y + y
        found = [pad_ref[located_ref[j, x, y]] for j in range(n_slots)]
        flat = [a_ref[pl.ds(j * 8 * rows_y + y, 8, stride=rows_y), :] for j in range(n_slots)]
        lhs = []
        for g in range(2):
            group = flat[g * 4 : g * 4 + 4]
            rolled = []
            for d in range(4):
                mixed = pick([group[(u + d) % 4] for u in range(4)])
                rolled.append(mixed if d == 0 else pltpu.roll(mixed, 32 * d, 1))
            lhs.append(
                jnp.concatenate([pick([rolled[(j - u) % 4] for j in range(4)]) for u in range(4)], axis=0)
            )
        tail = jnp.concatenate(
            [flat[8]] + [pltpu.roll(flat[8], 128 - 32 * u, 1) for u in range(1, 4)], axis=0
        )
        total = jnp.dot(
            jnp.concatenate(lhs, axis=1).astype(bf16),
            jnp.concatenate(found[0:8], axis=0),
            preferred_element_type=f32,
        )
        total += jnp.dot(tail[:, 0:n_units].astype(bf16), found[8], preferred_element_type=f32)
        for u in range(4):
            near_ref[p, pl.ds(u, 8, stride=4), :] = total[u * 8 : u * 8 + 8]

    def one_row(x, carry):
        for j in range(n_slots):
            for q in range(8):
                at = (j * 8 + q) * rows_y
                a_ref[at : at + rows_y, :] = nb_ref[x, j, :, q * 128 : (q + 1) * 128].astype(f32)

        def some(g, inner):
            for i in range(4):
                one_patch(x, g * 4 + i)
            return inner

        return lax.fori_loop(0, rows_y // 4, some, carry)

    lax.fori_loop(first, last, one_row, 0)


def far_part(perm_ref, slot_ref, lf_ref, dis_ref, cos_ref, sin_ref, near_ref, out_ref, far_ref):
    n_sub, n_box, _, quarter, n_sides = lf_ref.shape
    n_patch, n_dirs = cos_ref.shape
    n_units = near_ref.shape[1]
    per_box = n_patch // n_box

    dis_re, dis_im = dis_ref[0].astype(f32), dis_ref[1].astype(f32)

    def one_box(b):
        rows_d = []
        for i in range(per_box):
            p = perm_ref[b * per_box + i]
            c = cos_ref[pl.ds(p, 1), :]
            s = sin_ref[pl.ds(p, 1), :]
            rows_d.append(
                jnp.concatenate([c * dis_re - s * dis_im, s * dis_re + c * dis_im], axis=1).astype(bf16)
            )
        field = jnp.concatenate([lf_ref[q, b, c] for c in range(2) for q in range(n_sub)], axis=0)
        far = jnp.dot(jnp.concatenate(rows_d, axis=0), field, preferred_element_type=f32)
        for i in range(per_box):
            far_ref[b * per_box + i] = far[i * n_units : (i + 1) * n_units]

    def two_boxes(h, carry):
        one_box(2 * h)
        one_box(2 * h + 1)
        return carry

    lax.fori_loop(0, n_box // 2, two_boxes, 0)

    def some_patches(h, carry):
        for i in range(8):
            p = h * 8 + i
            out_ref[p] = (near_ref[p] + far_ref[slot_ref[p]]).astype(bf16)
        return carry

    lax.fori_loop(0, n_patch // 8, some_patches, 0)


def fused(
    n_strip, n_sub,
    perm_ref, slot_ref, index_in, cur_in, nb_in, angle_in, agg_in, dis_in, centre_in, shift_in,
    out_ref,
    index_ref, cur_ref, nb_ref, angle_ref, agg_ref, dis_ref, centre_ref, shift_ref, load_sem,
    pad_ref, box_ref, cos_ref, sin_ref, near_ref, a_ref, far_ref, lf_ref,
    cen_ref, shf_ref, in_ref, wide_ref, w_ref, inc_ref, exp_ref, coef_ref, send_ref, place_ref, located_ref, place_sem,
    halo_send, halo_recv, cen_send, cen_recv, shf_send, shf_recv, a2a_send, a2a_recv,
    exp_send, exp_recv, back_send, back_recv,
):
    strip = lax.axis_index("strip")
    sub = lax.axis_index("sub")
    rows_x, rows_y = cur_ref.shape[0], cur_ref.shape[1]
    n_units, n_sides = cur_ref.shape[2], cur_ref.shape[3]
    n_patch = rows_x * rows_y
    n_dirs = angle_ref.shape[1]
    quarter = n_dirs // n_sub
    n_box = centre_ref.shape[1]
    all_box = n_box * n_sub
    wide_y = rows_y + 2

    def sub_peer(d):
        return lax.rem(sub + d, n_sub)

    def strip_peer(d):
        return lax.rem(strip + d, n_strip)

    offsets = [(dx, dy) for dx in (-1, 0, 1) for dy in (-1, 0, 1) if dx or dy]

    pairs = [
        (index_in, index_ref), (centre_in, centre_ref), (shift_in, shift_ref), (cur_in, cur_ref),
        (angle_in, angle_ref), (agg_in, agg_ref), (nb_in, nb_ref), (dis_in, dis_ref),
    ]
    loads = [pltpu.make_async_copy(a, b, load_sem.at[i]) for i, (a, b) in enumerate(pairs)]
    for load in loads:
        load.start()

    barrier = pltpu.get_barrier_semaphore()
    for dx in (-1, 1):
        for dy in (-1, 1):
            pl.semaphore_signal(
                barrier, inc=1, device_id=(strip_peer(dx + n_strip), sub_peer(dy + n_sub)), device_id_type=MESH
            )
    for d in range(1, n_sub):
        pl.semaphore_signal(barrier, inc=1, device_id=(strip, sub_peer(d)), device_id_type=MESH)

    def greet(d, carry):
        pl.semaphore_signal(barrier, inc=1, device_id=(strip_peer(d), sub), device_id_type=MESH)
        return carry

    lax.fori_loop(1, n_strip, greet, 0)

    for load in loads[0:3]:
        load.wait()
    cen_ref[sub] = jnp.zeros((8, 128), f32)
    cen_ref[sub, 0:2, 0:n_box] = centre_ref[...]
    wanted = index_ref[...]
    ny_total = rows_y * n_sub
    row = wanted // ny_total
    place = (row - strip * rows_x + 1) * wide_y + (wanted - row * ny_total - sub * rows_y + 1)
    empty = (rows_x + 2) * wide_y
    place = jnp.minimum(jnp.maximum(place, 0), empty)
    place_ref[...] = jnp.where(wanted >= 0, place, empty)
    placing = pltpu.make_async_copy(place_ref, located_ref, place_sem)
    placing.start()
    shf_ref[strip] = jnp.zeros((8, n_dirs), f32)
    shf_ref[strip, 0:2, :] = shift_ref[0]
    pl.semaphore_wait(barrier, 4 + n_sub - 1 + n_strip - 1)

    def cen_copy(d):
        return pltpu.make_async_remote_copy(
            src_ref=cen_ref.at[sub], dst_ref=cen_ref.at[sub],
            send_sem=cen_send.at[d], recv_sem=cen_recv.at[d],
            device_id=(strip, sub_peer(d)), device_id_type=MESH,
        )

    def cen_wait(d):
        src = lax.rem(sub + n_sub - d, n_sub)
        return pltpu.make_async_remote_copy(
            src_ref=cen_ref.at[src], dst_ref=cen_ref.at[src],
            send_sem=cen_send.at[d], recv_sem=cen_recv.at[d],
            device_id=(strip, sub_peer(d)), device_id_type=MESH,
        )

    def strip_copy(buf, send, recv, d, at):
        return pltpu.make_async_remote_copy(
            src_ref=buf.at[at], dst_ref=buf.at[at],
            send_sem=send.at[d], recv_sem=recv.at[d],
            device_id=(strip_peer(d), sub), device_id_type=MESH,
        )

    def halo_copy(n):
        dx, dy = offsets[n]
        src_x = {-1: slice(0, 1), 0: slice(0, rows_x), 1: slice(rows_x - 1, rows_x)}[dx]
        src_y = {-1: slice(0, 1), 0: slice(0, rows_y), 1: slice(rows_y - 1, rows_y)}[dy]
        dst_x = {-1: slice(rows_x + 1, rows_x + 2), 0: slice(1, rows_x + 1), 1: slice(0, 1)}[dx]
        dst_y = {-1: slice(rows_y + 1, rows_y + 2), 0: slice(1, rows_y + 1), 1: slice(0, 1)}[dy]
        return pltpu.make_async_remote_copy(
            src_ref=cur_ref.at[src_x, src_y], dst_ref=pad_ref.at[dst_x, dst_y],
            send_sem=halo_send.at[n], recv_sem=halo_recv.at[n],
            device_id=(strip_peer(dx + n_strip), sub_peer(dy + n_sub)), device_id_type=MESH,
        )

    loads[3].wait()
    for d in range(1, n_sub):
        cen_copy(d).start()

    def send_shift(d, carry):
        strip_copy(shf_ref, shf_send, shf_recv, d, strip).start()
        return carry

    lax.fori_loop(1, n_strip, send_shift, 0)
    for n in range(len(offsets)):
        halo_copy(n).start()

    loads[4].wait()
    loads[5].wait()
    flat_cur = cur_ref.reshape(n_patch, n_units, n_sides)
    flat_pad = pad_ref.reshape((rows_x + 3) * wide_y, n_units, n_sides)

    gather_boxes(perm_ref, flat_cur, angle_ref, agg_ref, box_ref, cos_ref, sin_ref)

    def a2a_copy(d):
        return pltpu.make_async_remote_copy(
            src_ref=box_ref.at[sub_peer(d)], dst_ref=in_ref.at[d],
            send_sem=a2a_send.at[d], recv_sem=a2a_recv.at[d],
            device_id=(strip, sub_peer(d)), device_id_type=MESH,
        )

    for d in range(1, n_sub):
        a2a_copy(d).start()

    for x in range(rows_x):
        pad_ref[x + 1, 1 : rows_y + 1] = cur_ref[x]
    pad_ref[rows_x + 2, 0] = jnp.zeros((n_units, n_sides), bf16)

    def wait_shift(d, carry):
        src = lax.rem(strip + n_strip - d, n_strip)
        strip_copy(shf_ref, shf_send, shf_recv, d, src).wait_recv()
        return carry

    lax.fori_loop(1, n_strip, wait_shift, 0)
    for d in range(1, n_sub):
        cen_wait(d).wait_recv()
    one = jnp.ones((1, n_dirs), f32)
    zero = jnp.zeros((1, n_dirs), f32)

    def times(a, b):
        return a[0] * b[0] - a[1] * b[1], a[0] * b[1] + a[1] * b[0]

    coef = [None] * n_strip
    run = (one, zero)
    for q in reversed(range(n_strip)):
        t = (shf_ref[q, 0:1, :], shf_ref[q, 1:2, :])
        coef[q] = tuple(jnp.where(q < strip, part, 0.0) for part in run)
        run = times((jnp.where(q <= strip, t[0], 1.0), jnp.where(q <= strip, t[1], 0.0)), run)
    run = (one, zero)
    for q in range(n_strip):
        t = (shf_ref[q, 0:1, :], -shf_ref[q, 1:2, :])
        coef[q] = tuple(a + jnp.where(q > strip, part, 0.0) for a, part in zip(coef[q], run))
        run = times((jnp.where(q >= strip, t[0], 1.0), jnp.where(q >= strip, t[1], 0.0)), run)
    stacked = jnp.concatenate([c[0] for c in coef] + [c[1] for c in coef], axis=0)
    coef_ref[...] = stacked.T
    here = coef_ref[pl.ds(pl.multiple_of(sub * quarter, quarter), quarter), :]

    cen_row = jnp.concatenate([cen_ref[i, :, 0:n_box] for i in range(n_sub)], axis=1)
    cen_col = jnp.concatenate([cen_ref[i].T[0:n_box, :] for i in range(n_sub)], axis=0)
    col_x, col_y = cen_col[:, 0:1], cen_col[:, 1:2]
    row_x, row_y = cen_row[0:1, :], cen_row[1:2, :]
    step = 2.0 * math.pi / n_dirs
    k_col = lax.broadcasted_iota(jnp.int32, (quarter, all_box), 0) + sub * quarter
    angle = k_col.astype(f32) * step
    mid_x = (strip.astype(f32) + 0.5) * rows_x
    mid_y = 0.5 * rows_y * n_sub
    psi = wave_number * ((row_x - mid_x) * jnp.cos(angle) + (row_y - mid_y) * jnp.sin(angle))
    psi_re, psi_im = jnp.cos(psi), jnp.sin(psi)

    fold = 128 // all_box
    dx = col_x - jnp.concatenate([row_x] * fold, axis=1)
    dy = col_y - jnp.concatenate([row_y] * fold, axis=1)
    rho = jnp.sqrt(dx * dx + dy * dy)
    lane = lax.broadcasted_iota(jnp.int32, (all_box, 128), 1)
    target = lax.broadcasted_iota(jnp.int32, (all_box, 128), 0)
    amplitude = jnp.where(lane % all_box != target, 1.0 / (1.0 + rho), 0.0)
    lane_k = lax.broadcasted_iota(jnp.int32, (1, 128), 1) // all_box

    def weights(g, carry):
        turn = (lane_k + g * fold + sub * quarter).astype(f32) * step
        arg = wave_number * (rho + jnp.cos(turn) * dx + jnp.sin(turn) * dy)
        w_re = (amplitude * jnp.cos(arg)).astype(bf16).astype(f32)
        w_im = (amplitude * jnp.sin(arg)).astype(bf16).astype(f32)
        for i in range(fold):
            part = slice(i * all_box, (i + 1) * all_box)
            a, b = w_re[:, part], w_im[:, part]
            w_ref[g * fold + i] = jnp.concatenate(
                [jnp.concatenate([a, -b], axis=1), jnp.concatenate([b, a], axis=1)], axis=0
            ).astype(bf16)
        return carry

    lax.fori_loop(0, quarter // fold, weights, 0)

    placing.wait()
    loads[6].wait()
    loads[7].wait()
    for n in range(len(offsets)):
        halo_copy(n).wait_recv()
    split = NSPLIT * rows_x // 4
    later = LATER * rows_x // 4
    near_part(0, split, located_ref, nb_ref, flat_pad, near_ref, a_ref)

    def source(d):
        return lax.rem(sub + n_sub - d, n_sub)

    for d in range(n_sub):
        if d:
            a2a_copy(d).wait_recv()
        base = source(d)
        for b in range(n_box):
            for c in range(2):
                block = box_ref[sub, b, c] if d == 0 else in_ref[d, b, c]
                at = (c * all_box + base * n_box + b) * quarter
                wide_ref[pl.ds(pl.multiple_of(at, quarter), quarter), :] = block.astype(f32)

    total_re = jnp.zeros((quarter, n_sides), f32)
    total_im = jnp.zeros((quarter, n_sides), f32)
    for b in range(all_box):
        p_re, p_im = psi_re[:, b : b + 1], psi_im[:, b : b + 1]
        v_re = wide_ref[b * quarter : (b + 1) * quarter, :]
        v_im = wide_ref[(all_box + b) * quarter : (all_box + b + 1) * quarter, :]
        total_re += p_re * v_re - p_im * v_im
        total_im += p_im * v_re + p_re * v_im
    exp_ref[strip, 0] = (strip_weight * total_re).astype(bf16)
    exp_ref[strip, 1] = (strip_weight * total_im).astype(bf16)

    def send_exp(d, carry):
        strip_copy(exp_ref, exp_send, exp_recv, d, strip).start()
        return carry

    lax.fori_loop(1, n_strip, send_exp, 0)

    def interact(g, carry):
        ks = [g * 8 + i for i in range(8)]
        rhs = [wide_ref[pl.ds(k, 2 * all_box, stride=quarter), :].astype(bf16) for k in ks]
        out = [jnp.dot(w_ref[k], v, preferred_element_type=f32) for k, v in zip(ks, rhs)]
        for k, v in zip(ks, out):
            inc_ref[pl.ds(k, 2 * all_box, stride=quarter), :] = v
        return carry

    lax.fori_loop(0, quarter // 8, interact, 0)

    def wait_exp(d, carry):
        src = lax.rem(strip + n_strip - d, n_strip)
        strip_copy(exp_ref, exp_send, exp_recv, d, src).wait_recv()
        return carry

    near_part(split, later, located_ref, nb_ref, flat_pad, near_ref, a_ref)
    lax.fori_loop(1, n_strip, wait_exp, 0)
    field_re = jnp.zeros((quarter, n_sides), f32)
    field_im = jnp.zeros((quarter, n_sides), f32)
    for q in range(n_strip):
        c_re, c_im = here[:, q : q + 1], here[:, n_strip + q : n_strip + q + 1]
        v_re, v_im = exp_ref[q, 0].astype(f32), exp_ref[q, 1].astype(f32)
        field_re += c_re * v_re - c_im * v_im
        field_im += c_re * v_im + c_im * v_re
    def back_copy(d, at, to):
        return pltpu.make_async_remote_copy(
            src_ref=send_ref.at[to], dst_ref=lf_ref.at[at],
            send_sem=back_send.at[d], recv_sem=back_recv.at[d],
            device_id=(strip, to), device_id_type=MESH,
        )

    for b in range(all_box):
        p_re, p_im = psi_re[:, b : b + 1], psi_im[:, b : b + 1]
        v_re = inc_ref[b * quarter : (b + 1) * quarter, :]
        v_im = inc_ref[(all_box + b) * quarter : (all_box + b + 1) * quarter, :]
        send_ref[b // n_box, b % n_box, 0] = (v_re + p_re * field_re + p_im * field_im).astype(bf16)
        send_ref[b // n_box, b % n_box, 1] = (v_im + p_re * field_im - p_im * field_re).astype(bf16)
        if b % n_box == n_box - 1:
            to = b // n_box

            @pl.when(to != sub)
            def _(to=to):
                back_copy(lax.rem(to - sub + n_sub, n_sub), sub, to).start()


    lf_ref[sub] = send_ref[sub]

    near_part(later, rows_x, located_ref, nb_ref, flat_pad, near_ref, a_ref)

    for d in range(1, n_sub):
        back_copy(d, source(d), sub_peer(d)).wait_recv()
    far_part(perm_ref, slot_ref, lf_ref, dis_ref, cos_ref, sin_ref, near_ref, out_ref, far_ref)

    for d in range(1, n_sub):
        cen_copy(d).wait_send()
        a2a_copy(d).wait_send()
        back_copy(d, sub, sub_peer(d)).wait_send()

    def drain(d, carry):
        strip_copy(shf_ref, shf_send, shf_recv, d, strip).wait_send()
        strip_copy(exp_ref, exp_send, exp_recv, d, strip).wait_send()
        return carry

    lax.fori_loop(1, n_strip, drain, 0)
    for n in range(len(offsets)):
        halo_copy(n).wait_send()


def per_device(
    currents,
    near_blocks,
    near_index,
    box_of_patch,
    box_centre,
    patch_angle,
    aggregation,
    disaggregation,
    strip_shift,
):
    rows_x, rows_y, n_units, n_sides = currents.shape
    n_dirs = patch_angle.shape[2]
    n_slots = near_index.shape[2]
    n_patch = rows_x * rows_y
    box_dev = box_centre.shape[0]
    n_sub = lax.axis_size("sub")
    n_strip = lax.axis_size("strip")
    quarter = n_dirs // n_sub
    all_box = box_dev * n_sub
    ids = jnp.arange(n_patch, dtype=jnp.int32)
    key = box_of_patch.reshape(n_patch) * n_patch + ids
    slot = jnp.sum((key[None, :] < key[:, None]).astype(jnp.int32), axis=1)
    perm = jnp.sum(jnp.where(slot[None, :] == ids[:, None], ids[None, :], 0), axis=1)
    smem = pl.BlockSpec(memory_space=pltpu.SMEM)
    vmem = pl.BlockSpec(memory_space=pltpu.VMEM)
    dma = pltpu.SemaphoreType.DMA
    operands = (
        jnp.transpose(near_index, (2, 0, 1)),
        currents,
        jnp.transpose(near_blocks, (0, 2, 1, 3)),
        patch_angle.reshape(n_patch, n_dirs),
        jnp.swapaxes(aggregation, 1, 2),
        jnp.swapaxes(disaggregation, 1, 2),
        box_centre.T,
        strip_shift,
    )
    hbm = pl.BlockSpec(memory_space=pltpu.HBM)
    scratch = [pltpu.VMEM(a.shape, a.dtype) for a in operands] + [
        dma((8,)),
        pltpu.VMEM((rows_x + 3, rows_y + 2, n_units, n_sides), bf16),
        pltpu.VMEM((n_sub, box_dev, 2, quarter, n_sides), bf16),
        pltpu.VMEM((n_patch, n_dirs), f32),
        pltpu.VMEM((n_patch, n_dirs), f32),
        pltpu.VMEM((n_patch, n_units, n_sides), f32),
        pltpu.VMEM((n_slots * 8 * rows_y, 128), f32),
        pltpu.VMEM((n_patch, n_units, n_sides), f32),
        pltpu.VMEM((n_sub, box_dev, 2, quarter, n_sides), bf16),
        pltpu.VMEM((n_sub, 8, 128), f32),
        pltpu.VMEM((n_strip, 8, n_dirs), f32),
        pltpu.VMEM((n_sub, box_dev, 2, quarter, n_sides), bf16),
        pltpu.VMEM((2 * all_box * quarter, n_sides), f32),
        pltpu.VMEM((quarter, 2 * all_box, 2 * all_box), bf16),
        pltpu.VMEM((2 * all_box * quarter, n_sides), f32),
        pltpu.VMEM((n_strip, 2, quarter, n_sides), bf16),
        pltpu.VMEM((n_dirs, 2 * n_strip), f32),
        pltpu.VMEM((n_sub, box_dev, 2, quarter, n_sides), bf16),
        pltpu.VMEM((n_slots, rows_x, rows_y), jnp.int32),
        pltpu.SMEM((n_slots, rows_x, rows_y), jnp.int32),
        dma(()),
        dma((8,)), dma((8,)),
        dma((n_sub,)), dma((n_sub,)),
        dma((n_strip,)), dma((n_strip,)),
        dma((n_sub,)), dma((n_sub,)),
        dma((n_strip,)), dma((n_strip,)),
        dma((n_sub,)), dma((n_sub,)),
    ]
    result = pl.pallas_call(
        functools.partial(fused, n_strip, n_sub),
        out_shape=jax.ShapeDtypeStruct((n_patch, n_units, n_sides), bf16),
        in_specs=[smem] * 2 + [hbm] * 8,
        out_specs=vmem,
        scratch_shapes=scratch,
        compiler_params=pltpu.CompilerParams(
            collective_id=0, has_side_effects=True, vmem_limit_bytes=60 * 1024 * 1024
        ),
    )(
        perm,
        slot,
        *operands,
    )
    return result.reshape(rows_x, rows_y, n_units, n_sides)


def solution(mesh):
    in_specs = (
        P("strip", "sub", None, None),
        P("strip", "sub", None, None),
        P("strip", "sub", None),
        P("strip", "sub"),
        P(("strip", "sub"), None),
        P("strip", "sub", None),
        P(),
        P(),
        P("strip", None, None),
    )
    out_specs = P("strip", "sub", None, None)
    return jax.shard_map(
        per_device, mesh=mesh, in_specs=in_specs, out_specs=out_specs, check_vma=False
    )
```

```python
import functools
import math

import jax
import jax.numpy as jnp
from jax import lax
from jax.experimental import pallas as pl
from jax.experimental.pallas import tpu as pltpu
from jax.sharding import PartitionSpec as P

wave_number = 1.5
strip_weight = 0.03
MESH = pl.DeviceIdType.MESH
f32 = jnp.float32
bf16 = jnp.bfloat16


def gather_boxes(perm_ref, cur_ref, angle_ref, agg_ref, box_ref, cos_ref, sin_ref):
    n_sub, n_box, _, quarter, _ = box_ref.shape
    n_patch, n_dirs = angle_ref.shape
    n_units = cur_ref.shape[1]
    per_box = n_patch // n_box
    cos_ref[...] = jnp.cos(angle_ref[...])
    sin_ref[...] = jnp.sin(angle_ref[...])

    agg_re, agg_im = agg_ref[0].astype(f32), agg_ref[1].astype(f32)

    def one_box(b):
        rows_e, rows_x = [], []
        for i in range(per_box):
            p = perm_ref[b * per_box + i]
            rows_x.append(cur_ref[p])
            c = cos_ref[pl.ds(p, 1), :]
            s = sin_ref[pl.ds(p, 1), :]
            rows_e.append(
                jnp.concatenate([c * agg_re - s * agg_im, s * agg_re + c * agg_im], axis=1).astype(bf16)
            )
        values = lax.dot_general(
            jnp.concatenate(rows_e, axis=0),
            jnp.concatenate(rows_x, axis=0),
            (((0,), (0,)), ((), ())),
            preferred_element_type=f32,
        ).astype(bf16)
        for c in range(2):
            for q in range(n_sub):
                at = c * n_dirs + q * quarter
                box_ref[q, b, c] = values[at : at + quarter]

    def two_boxes(h, carry):
        one_box(2 * h)
        one_box(2 * h + 1)
        return carry

    lax.fori_loop(0, n_box // 2, two_boxes, 0)


def near_part(first, last, located_ref, nb_ref, pad_ref, near_ref, a_ref):
    _, n_slots, rows_y, _ = nb_ref.shape
    n_units, n_sides = near_ref.shape[1:]
    lanes = lax.broadcasted_iota(jnp.int32, (8, 128), 1) // 32

    def pick(parts):
        out = parts[0]
        for i in range(1, 4):
            out = jnp.where(lanes == i, parts[i], out)
        return out

    def one_patch(x, y):
        p = x * rows_y + y
        found = [pad_ref[located_ref[j, x, y]] for j in range(n_slots)]
        flat = [a_ref[pl.ds(j * 8 * rows_y + y, 8, stride=rows_y), :] for j in range(n_slots)]
        lhs = []
        for g in range(2):
            group = flat[g * 4 : g * 4 + 4]
            rolled = []
            for d in range(4):
                mixed = pick([group[(u + d) % 4] for u in range(4)])
                rolled.append(mixed if d == 0 else pltpu.roll(mixed, 32 * d, 1))
            lhs.append(
                jnp.concatenate([pick([rolled[(j - u) % 4] for j in range(4)]) for u in range(4)], axis=0)
            )
        tail = jnp.concatenate(
            [flat[8]] + [pltpu.roll(flat[8], 128 - 32 * u, 1) for u in range(1, 4)], axis=0
        )
        total = jnp.dot(
            jnp.concatenate(lhs, axis=1).astype(bf16),
            jnp.concatenate(found[0:8], axis=0),
            preferred_element_type=f32,
        )
        total += jnp.dot(tail[:, 0:n_units].astype(bf16), found[8], preferred_element_type=f32)
        for u in range(4):
            near_ref[p, pl.ds(u, 8, stride=4), :] = total[u * 8 : u * 8 + 8]

    def one_row(x, carry):
        for j in range(n_slots):
            for q in range(8):
                at = (j * 8 + q) * rows_y
                a_ref[at : at + rows_y, :] = nb_ref[x, j, :, q * 128 : (q + 1) * 128].astype(f32)

        def some(g, inner):
            for i in range(4):
                one_patch(x, g * 4 + i)
            return inner

        return lax.fori_loop(0, rows_y // 4, some, carry)

    lax.fori_loop(first, last, one_row, 0)


def far_part(perm_ref, slot_ref, lf_ref, dis_ref, cos_ref, sin_ref, near_ref, out_ref, far_ref):
    n_sub, n_box, _, quarter, n_sides = lf_ref.shape
    n_patch, n_dirs = cos_ref.shape
    n_units = near_ref.shape[1]
    per_box = n_patch // n_box

    dis_re, dis_im = dis_ref[0].astype(f32), dis_ref[1].astype(f32)

    def one_box(b):
        rows_d = []
        for i in range(per_box):
            p = perm_ref[b * per_box + i]
            c = cos_ref[pl.ds(p, 1), :]
            s = sin_ref[pl.ds(p, 1), :]
            rows_d.append(
                jnp.concatenate([c * dis_re - s * dis_im, s * dis_re + c * dis_im], axis=1).astype(bf16)
            )
        field = jnp.concatenate([lf_ref[q, b, c] for c in range(2) for q in range(n_sub)], axis=0)
        far = jnp.dot(jnp.concatenate(rows_d, axis=0), field, preferred_element_type=f32)
        for i in range(per_box):
            far_ref[b * per_box + i] = far[i * n_units : (i + 1) * n_units]

    def two_boxes(h, carry):
        one_box(2 * h)
        one_box(2 * h + 1)
        return carry

    lax.fori_loop(0, n_box // 2, two_boxes, 0)

    def some_patches(h, carry):
        for i in range(8):
            p = h * 8 + i
            out_ref[p] = (near_ref[p] + far_ref[slot_ref[p]]).astype(bf16)
        return carry

    lax.fori_loop(0, n_patch // 8, some_patches, 0)


def fused(
    n_strip, n_sub,
    perm_ref, slot_ref, index_in, cur_in, nb_in, angle_in, agg_in, dis_in, centre_in, shift_in,
    out_ref,
    index_ref, cur_ref, nb_ref, angle_ref, agg_ref, dis_ref, centre_ref, shift_ref, load_sem,
    pad_ref, box_ref, cos_ref, sin_ref, near_ref, a_ref, far_ref, lf_ref,
    cen_ref, shf_ref, in_ref, wide_ref, w_ref, inc_ref, exp_ref, coef_ref, send_ref, place_ref, located_ref, place_sem,
    halo_send, halo_recv, cen_send, cen_recv, shf_send, shf_recv, a2a_send, a2a_recv,
    exp_send, exp_recv, back_send, back_recv,
):
    strip = lax.axis_index("strip")
    sub = lax.axis_index("sub")
    rows_x, rows_y = cur_ref.shape[0], cur_ref.shape[1]
    n_units, n_sides = cur_ref.shape[2], cur_ref.shape[3]
    n_patch = rows_x * rows_y
    n_dirs = angle_ref.shape[1]
    quarter = n_dirs // n_sub
    n_box = centre_ref.shape[1]
    all_box = n_box * n_sub
    wide_y = rows_y + 2

    def sub_peer(d):
        return lax.rem(sub + d, n_sub)

    def strip_peer(d):
        return lax.rem(strip + d, n_strip)

    offsets = [(dx, dy) for dx in (-1, 0, 1) for dy in (-1, 0, 1) if dx or dy]

    pairs = [
        (index_in, index_ref), (centre_in, centre_ref), (shift_in, shift_ref), (cur_in, cur_ref),
        (angle_in, angle_ref), (agg_in, agg_ref), (nb_in, nb_ref), (dis_in, dis_ref),
    ]
    loads = [pltpu.make_async_copy(a, b, load_sem.at[i]) for i, (a, b) in enumerate(pairs)]
    for load in loads:
        load.start()

    barrier = pltpu.get_barrier_semaphore()
    for dx in (-1, 1):
        for dy in (-1, 1):
            pl.semaphore_signal(
                barrier, inc=1, device_id=(strip_peer(dx + n_strip), sub_peer(dy + n_sub)), device_id_type=MESH
            )
    for d in range(1, n_sub):
        pl.semaphore_signal(barrier, inc=1, device_id=(strip, sub_peer(d)), device_id_type=MESH)

    def greet(d, carry):
        pl.semaphore_signal(barrier, inc=1, device_id=(strip_peer(d), sub), device_id_type=MESH)
        return carry

    lax.fori_loop(1, n_strip, greet, 0)

    for load in loads[0:3]:
        load.wait()
    cen_ref[sub] = jnp.zeros((8, 128), f32)
    cen_ref[sub, 0:2, 0:n_box] = centre_ref[...]
    wanted = index_ref[...]
    ny_total = rows_y * n_sub
    row = wanted // ny_total
    place = (row - strip * rows_x + 1) * wide_y + (wanted - row * ny_total - sub * rows_y + 1)
    empty = (rows_x + 2) * wide_y
    place = jnp.minimum(jnp.maximum(place, 0), empty)
    place_ref[...] = jnp.where(wanted >= 0, place, empty)
    placing = pltpu.make_async_copy(place_ref, located_ref, place_sem)
    placing.start()
    shf_ref[strip] = jnp.zeros((8, n_dirs), f32)
    shf_ref[strip, 0:2, :] = shift_ref[0]
    pl.semaphore_wait(barrier, 4 + n_sub - 1 + n_strip - 1)

    def cen_copy(d):
        return pltpu.make_async_remote_copy(
            src_ref=cen_ref.at[sub], dst_ref=cen_ref.at[sub],
            send_sem=cen_send.at[d], recv_sem=cen_recv.at[d],
            device_id=(strip, sub_peer(d)), device_id_type=MESH,
        )

    def cen_wait(d):
        src = lax.rem(sub + n_sub - d, n_sub)
        return pltpu.make_async_remote_copy(
            src_ref=cen_ref.at[src], dst_ref=cen_ref.at[src],
            send_sem=cen_send.at[d], recv_sem=cen_recv.at[d],
            device_id=(strip, sub_peer(d)), device_id_type=MESH,
        )

    def strip_copy(buf, send, recv, d, at):
        return pltpu.make_async_remote_copy(
            src_ref=buf.at[at], dst_ref=buf.at[at],
            send_sem=send.at[d], recv_sem=recv.at[d],
            device_id=(strip_peer(d), sub), device_id_type=MESH,
        )

    def halo_copy(n):
        dx, dy = offsets[n]
        src_x = {-1: slice(0, 1), 0: slice(0, rows_x), 1: slice(rows_x - 1, rows_x)}[dx]
        src_y = {-1: slice(0, 1), 0: slice(0, rows_y), 1: slice(rows_y - 1, rows_y)}[dy]
        dst_x = {-1: slice(rows_x + 1, rows_x + 2), 0: slice(1, rows_x + 1), 1: slice(0, 1)}[dx]
        dst_y = {-1: slice(rows_y + 1, rows_y + 2), 0: slice(1, rows_y + 1), 1: slice(0, 1)}[dy]
        return pltpu.make_async_remote_copy(
            src_ref=cur_ref.at[src_x, src_y], dst_ref=pad_ref.at[dst_x, dst_y],
            send_sem=halo_send.at[n], recv_sem=halo_recv.at[n],
            device_id=(strip_peer(dx + n_strip), sub_peer(dy + n_sub)), device_id_type=MESH,
        )

    loads[3].wait()
    for d in range(1, n_sub):
        cen_copy(d).start()

    def send_shift(d, carry):
        strip_copy(shf_ref, shf_send, shf_recv, d, strip).start()
        return carry

    lax.fori_loop(1, n_strip, send_shift, 0)

    loads[4].wait()
    loads[5].wait()
    flat_cur = cur_ref.reshape(n_patch, n_units, n_sides)
    flat_pad = pad_ref.reshape((rows_x + 3) * wide_y, n_units, n_sides)

    gather_boxes(perm_ref, flat_cur, angle_ref, agg_ref, box_ref, cos_ref, sin_ref)

    def a2a_copy(d):
        return pltpu.make_async_remote_copy(
            src_ref=box_ref.at[sub_peer(d)], dst_ref=in_ref.at[d],
            send_sem=a2a_send.at[d], recv_sem=a2a_recv.at[d],
            device_id=(strip, sub_peer(d)), device_id_type=MESH,
        )

    for d in range(1, n_sub):
        a2a_copy(d).start()
    for n in range(len(offsets)):
        halo_copy(n).start()

    for x in range(rows_x):
        pad_ref[x + 1, 1 : rows_y + 1] = cur_ref[x]
    pad_ref[rows_x + 2, 0] = jnp.zeros((n_units, n_sides), bf16)

    def wait_shift(d, carry):
        src = lax.rem(strip + n_strip - d, n_strip)
        strip_copy(shf_ref, shf_send, shf_recv, d, src).wait_recv()
        return carry

    lax.fori_loop(1, n_strip, wait_shift, 0)
    for d in range(1, n_sub):
        cen_wait(d).wait_recv()
    one = jnp.ones((1, n_dirs), f32)
    zero = jnp.zeros((1, n_dirs), f32)

    def times(a, b):
        return a[0] * b[0] - a[1] * b[1], a[0] * b[1] + a[1] * b[0]

    coef = [None] * n_strip
    run = (one, zero)
    for q in reversed(range(n_strip)):
        t = (shf_ref[q, 0:1, :], shf_ref[q, 1:2, :])
        coef[q] = tuple(jnp.where(q < strip, part, 0.0) for part in run)
        run = times((jnp.where(q <= strip, t[0], 1.0), jnp.where(q <= strip, t[1], 0.0)), run)
    run = (one, zero)
    for q in range(n_strip):
        t = (shf_ref[q, 0:1, :], -shf_ref[q, 1:2, :])
        coef[q] = tuple(a + jnp.where(q > strip, part, 0.0) for a, part in zip(coef[q], run))
        run = times((jnp.where(q >= strip, t[0], 1.0), jnp.where(q >= strip, t[1], 0.0)), run)
    stacked = jnp.concatenate([c[0] for c in coef] + [c[1] for c in coef], axis=0)
    coef_ref[...] = stacked.T
    here = coef_ref[pl.ds(pl.multiple_of(sub * quarter, quarter), quarter), :]

    cen_row = jnp.concatenate([cen_ref[i, :, 0:n_box] for i in range(n_sub)], axis=1)
    cen_col = jnp.concatenate([cen_ref[i].T[0:n_box, :] for i in range(n_sub)], axis=0)
    col_x, col_y = cen_col[:, 0:1], cen_col[:, 1:2]
    row_x, row_y = cen_row[0:1, :], cen_row[1:2, :]
    step = 2.0 * math.pi / n_dirs
    k_col = lax.broadcasted_iota(jnp.int32, (quarter, all_box), 0) + sub * quarter
    angle = k_col.astype(f32) * step
    mid_x = (strip.astype(f32) + 0.5) * rows_x
    mid_y = 0.5 * rows_y * n_sub
    psi = wave_number * ((row_x - mid_x) * jnp.cos(angle) + (row_y - mid_y) * jnp.sin(angle))
    psi_re, psi_im = jnp.cos(psi), jnp.sin(psi)

    fold = 128 // all_box
    dx = col_x - jnp.concatenate([row_x] * fold, axis=1)
    dy = col_y - jnp.concatenate([row_y] * fold, axis=1)
    rho = jnp.sqrt(dx * dx + dy * dy)
    lane = lax.broadcasted_iota(jnp.int32, (all_box, 128), 1)
    target = lax.broadcasted_iota(jnp.int32, (all_box, 128), 0)
    amplitude = jnp.where(lane % all_box != target, 1.0 / (1.0 + rho), 0.0)
    lane_k = lax.broadcasted_iota(jnp.int32, (1, 128), 1) // all_box

    def weights(g, carry):
        turn = (lane_k + g * fold + sub * quarter).astype(f32) * step
        arg = wave_number * (rho + jnp.cos(turn) * dx + jnp.sin(turn) * dy)
        w_re = (amplitude * jnp.cos(arg)).astype(bf16).astype(f32)
        w_im = (amplitude * jnp.sin(arg)).astype(bf16).astype(f32)
        for i in range(fold):
            part = slice(i * all_box, (i + 1) * all_box)
            a, b = w_re[:, part], w_im[:, part]
            w_ref[g * fold + i] = jnp.concatenate(
                [jnp.concatenate([a, -b], axis=1), jnp.concatenate([b, a], axis=1)], axis=0
            ).astype(bf16)
        return carry

    lax.fori_loop(0, quarter // fold, weights, 0)

    placing.wait()
    loads[6].wait()
    loads[7].wait()

    def source(d):
        return lax.rem(sub + n_sub - d, n_sub)

    for d in range(n_sub):
        if d:
            a2a_copy(d).wait_recv()
        base = source(d)
        for b in range(n_box):
            for c in range(2):
                block = box_ref[sub, b, c] if d == 0 else in_ref[d, b, c]
                at = (c * all_box + base * n_box + b) * quarter
                wide_ref[pl.ds(pl.multiple_of(at, quarter), quarter), :] = block.astype(f32)

    total_re = jnp.zeros((quarter, n_sides), f32)
    total_im = jnp.zeros((quarter, n_sides), f32)
    for b in range(all_box):
        p_re, p_im = psi_re[:, b : b + 1], psi_im[:, b : b + 1]
        v_re = wide_ref[b * quarter : (b + 1) * quarter, :]
        v_im = wide_ref[(all_box + b) * quarter : (all_box + b + 1) * quarter, :]
        total_re += p_re * v_re - p_im * v_im
        total_im += p_im * v_re + p_re * v_im
    exp_ref[strip, 0] = (strip_weight * total_re).astype(bf16)
    exp_ref[strip, 1] = (strip_weight * total_im).astype(bf16)

    def send_exp(d, carry):
        strip_copy(exp_ref, exp_send, exp_recv, d, strip).start()
        return carry

    lax.fori_loop(1, n_strip, send_exp, 0)

    def interact(g, carry):
        ks = [g * 8 + i for i in range(8)]
        rhs = [wide_ref[pl.ds(k, 2 * all_box, stride=quarter), :].astype(bf16) for k in ks]
        out = [jnp.dot(w_ref[k], v, preferred_element_type=f32) for k, v in zip(ks, rhs)]
        for k, v in zip(ks, out):
            inc_ref[pl.ds(k, 2 * all_box, stride=quarter), :] = v
        return carry

    lax.fori_loop(0, quarter // 8, interact, 0)

    def wait_exp(d, carry):
        src = lax.rem(strip + n_strip - d, n_strip)
        strip_copy(exp_ref, exp_send, exp_recv, d, src).wait_recv()
        return carry

    lax.fori_loop(1, n_strip, wait_exp, 0)
    field_re = jnp.zeros((quarter, n_sides), f32)
    field_im = jnp.zeros((quarter, n_sides), f32)
    for q in range(n_strip):
        c_re, c_im = here[:, q : q + 1], here[:, n_strip + q : n_strip + q + 1]
        v_re, v_im = exp_ref[q, 0].astype(f32), exp_ref[q, 1].astype(f32)
        field_re += c_re * v_re - c_im * v_im
        field_im += c_re * v_im + c_im * v_re
    def back_copy(d, at, to):
        return pltpu.make_async_remote_copy(
            src_ref=send_ref.at[to], dst_ref=lf_ref.at[at],
            send_sem=back_send.at[d], recv_sem=back_recv.at[d],
            device_id=(strip, to), device_id_type=MESH,
        )

    for b in range(all_box):
        p_re, p_im = psi_re[:, b : b + 1], psi_im[:, b : b + 1]
        v_re = inc_ref[b * quarter : (b + 1) * quarter, :]
        v_im = inc_ref[(all_box + b) * quarter : (all_box + b + 1) * quarter, :]
        send_ref[b // n_box, b % n_box, 0] = (v_re + p_re * field_re + p_im * field_im).astype(bf16)
        send_ref[b // n_box, b % n_box, 1] = (v_im + p_re * field_im - p_im * field_re).astype(bf16)
        if b % n_box == n_box - 1:
            to = b // n_box

            @pl.when(to != sub)
            def _(to=to):
                back_copy(lax.rem(to - sub + n_sub, n_sub), sub, to).start()


    lf_ref[sub] = send_ref[sub]

    for n in range(len(offsets)):
        halo_copy(n).wait_recv()
    near_part(0, rows_x, located_ref, nb_ref, flat_pad, near_ref, a_ref)

    for d in range(1, n_sub):
        back_copy(d, source(d), sub_peer(d)).wait_recv()
    far_part(perm_ref, slot_ref, lf_ref, dis_ref, cos_ref, sin_ref, near_ref, out_ref, far_ref)

    for d in range(1, n_sub):
        cen_copy(d).wait_send()
        a2a_copy(d).wait_send()
        back_copy(d, sub, sub_peer(d)).wait_send()

    def drain(d, carry):
        strip_copy(shf_ref, shf_send, shf_recv, d, strip).wait_send()
        strip_copy(exp_ref, exp_send, exp_recv, d, strip).wait_send()
        return carry

    lax.fori_loop(1, n_strip, drain, 0)
    for n in range(len(offsets)):
        halo_copy(n).wait_send()


def per_device(
    currents,
    near_blocks,
    near_index,
    box_of_patch,
    box_centre,
    patch_angle,
    aggregation,
    disaggregation,
    strip_shift,
):
    rows_x, rows_y, n_units, n_sides = currents.shape
    n_dirs = patch_angle.shape[2]
    n_slots = near_index.shape[2]
    n_patch = rows_x * rows_y
    box_dev = box_centre.shape[0]
    n_sub = lax.axis_size("sub")
    n_strip = lax.axis_size("strip")
    quarter = n_dirs // n_sub
    all_box = box_dev * n_sub
    ids = jnp.arange(n_patch, dtype=jnp.int32)
    key = box_of_patch.reshape(n_patch) * n_patch + ids
    slot = jnp.sum((key[None, :] < key[:, None]).astype(jnp.int32), axis=1)
    perm = jnp.sum(jnp.where(slot[None, :] == ids[:, None], ids[None, :], 0), axis=1)
    smem = pl.BlockSpec(memory_space=pltpu.SMEM)
    vmem = pl.BlockSpec(memory_space=pltpu.VMEM)
    dma = pltpu.SemaphoreType.DMA
    operands = (
        jnp.transpose(near_index, (2, 0, 1)),
        currents,
        jnp.transpose(near_blocks, (0, 2, 1, 3)),
        patch_angle.reshape(n_patch, n_dirs),
        jnp.swapaxes(aggregation, 1, 2),
        jnp.swapaxes(disaggregation, 1, 2),
        box_centre.T,
        strip_shift,
    )
    hbm = pl.BlockSpec(memory_space=pltpu.HBM)
    scratch = [pltpu.VMEM(a.shape, a.dtype) for a in operands] + [
        dma((8,)),
        pltpu.VMEM((rows_x + 3, rows_y + 2, n_units, n_sides), bf16),
        pltpu.VMEM((n_sub, box_dev, 2, quarter, n_sides), bf16),
        pltpu.VMEM((n_patch, n_dirs), f32),
        pltpu.VMEM((n_patch, n_dirs), f32),
        pltpu.VMEM((n_patch, n_units, n_sides), f32),
        pltpu.VMEM((n_slots * 8 * rows_y, 128), f32),
        pltpu.VMEM((n_patch, n_units, n_sides), f32),
        pltpu.VMEM((n_sub, box_dev, 2, quarter, n_sides), bf16),
        pltpu.VMEM((n_sub, 8, 128), f32),
        pltpu.VMEM((n_strip, 8, n_dirs), f32),
        pltpu.VMEM((n_sub, box_dev, 2, quarter, n_sides), bf16),
        pltpu.VMEM((2 * all_box * quarter, n_sides), f32),
        pltpu.VMEM((quarter, 2 * all_box, 2 * all_box), bf16),
        pltpu.VMEM((2 * all_box * quarter, n_sides), f32),
        pltpu.VMEM((n_strip, 2, quarter, n_sides), bf16),
        pltpu.VMEM((n_dirs, 2 * n_strip), f32),
        pltpu.VMEM((n_sub, box_dev, 2, quarter, n_sides), bf16),
        pltpu.VMEM((n_slots, rows_x, rows_y), jnp.int32),
        pltpu.SMEM((n_slots, rows_x, rows_y), jnp.int32),
        dma(()),
        dma((8,)), dma((8,)),
        dma((n_sub,)), dma((n_sub,)),
        dma((n_strip,)), dma((n_strip,)),
        dma((n_sub,)), dma((n_sub,)),
        dma((n_strip,)), dma((n_strip,)),
        dma((n_sub,)), dma((n_sub,)),
    ]
    result = pl.pallas_call(
        functools.partial(fused, n_strip, n_sub),
        out_shape=jax.ShapeDtypeStruct((n_patch, n_units, n_sides), bf16),
        in_specs=[smem] * 2 + [hbm] * 8,
        out_specs=vmem,
        scratch_shapes=scratch,
        compiler_params=pltpu.CompilerParams(
            collective_id=0, has_side_effects=True, vmem_limit_bytes=60 * 1024 * 1024
        ),
    )(
        perm,
        slot,
        *operands,
    )
    return result.reshape(rows_x, rows_y, n_units, n_sides)


def solution(mesh):
    in_specs = (
        P("strip", "sub", None, None),
        P("strip", "sub", None, None),
        P("strip", "sub", None),
        P("strip", "sub"),
        P(("strip", "sub"), None),
        P("strip", "sub", None),
        P(),
        P(),
        P("strip", None, None),
    )
    out_specs = P("strip", "sub", None, None)
    return jax.shard_map(
        per_device, mesh=mesh, in_specs=in_specs, out_specs=out_specs, check_vma=False
    )
```

```python
import functools
import math

import jax
import jax.numpy as jnp
from jax import lax
from jax.experimental import pallas as pl
from jax.experimental.pallas import tpu as pltpu
from jax.sharding import PartitionSpec as P

wave_number = 1.5
strip_weight = 0.03
MESH = pl.DeviceIdType.MESH
f32 = jnp.float32
bf16 = jnp.bfloat16


def gather_boxes(perm_ref, cur_ref, angle_ref, agg_ref, box_ref, cos_ref, sin_ref):
    n_sub, n_box, _, quarter, _ = box_ref.shape
    n_patch, n_dirs = angle_ref.shape
    n_units = cur_ref.shape[1]
    per_box = n_patch // n_box
    cos_ref[...] = jnp.cos(angle_ref[...])
    sin_ref[...] = jnp.sin(angle_ref[...])

    agg_re, agg_im = agg_ref[0].astype(f32), agg_ref[1].astype(f32)

    def one_box(b):
        rows_e, rows_x = [], []
        for i in range(per_box):
            p = perm_ref[b * per_box + i]
            rows_x.append(cur_ref[p])
            c = cos_ref[pl.ds(p, 1), :]
            s = sin_ref[pl.ds(p, 1), :]
            rows_e.append(
                jnp.concatenate([c * agg_re - s * agg_im, s * agg_re + c * agg_im], axis=1).astype(bf16)
            )
        values = lax.dot_general(
            jnp.concatenate(rows_e, axis=0),
            jnp.concatenate(rows_x, axis=0),
            (((0,), (0,)), ((), ())),
            preferred_element_type=f32,
        ).astype(bf16)
        for c in range(2):
            for q in range(n_sub):
                at = c * n_dirs + q * quarter
                box_ref[q, b, c] = values[at : at + quarter]

    def two_boxes(h, carry):
        one_box(2 * h)
        one_box(2 * h + 1)
        return carry

    lax.fori_loop(0, n_box // 2, two_boxes, 0)


def near_part(first, last, located_ref, nb_ref, pad_ref, near_ref, a_ref):
    _, n_slots, rows_y, _ = nb_ref.shape
    n_units, n_sides = near_ref.shape[1:]
    lanes = lax.broadcasted_iota(jnp.int32, (8, 128), 1) // 32

    def pick(parts):
        out = parts[0]
        for i in range(1, 4):
            out = jnp.where(lanes == i, parts[i], out)
        return out

    def one_patch(x, y):
        p = x * rows_y + y
        found = [pad_ref[located_ref[j, x, y]] for j in range(n_slots)]
        flat = [a_ref[pl.ds(j * 8 * rows_y + y, 8, stride=rows_y), :] for j in range(n_slots)]
        lhs = []
        for g in range(2):
            group = flat[g * 4 : g * 4 + 4]
            rolled = []
            for d in range(4):
                mixed = pick([group[(u + d) % 4] for u in range(4)])
                rolled.append(mixed if d == 0 else pltpu.roll(mixed, 32 * d, 1))
            lhs.append(
                jnp.concatenate([pick([rolled[(j - u) % 4] for j in range(4)]) for u in range(4)], axis=0)
            )
        tail = jnp.concatenate(
            [flat[8]] + [pltpu.roll(flat[8], 128 - 32 * u, 1) for u in range(1, 4)], axis=0
        )
        total = jnp.dot(
            jnp.concatenate(lhs, axis=1).astype(bf16),
            jnp.concatenate(found[0:8], axis=0),
            preferred_element_type=f32,
        )
        total += jnp.dot(tail[:, 0:n_units].astype(bf16), found[8], preferred_element_type=f32)
        for u in range(4):
            near_ref[p, pl.ds(u, 8, stride=4), :] = total[u * 8 : u * 8 + 8]

    def one_row(x, carry):
        for j in range(n_slots):
            for q in range(8):
                at = (j * 8 + q) * rows_y
                a_ref[at : at + rows_y, :] = nb_ref[x, j, :, q * 128 : (q + 1) * 128].astype(f32)

        def some(g, inner):
            for i in range(4):
                one_patch(x, g * 4 + i)
            return inner

        return lax.fori_loop(0, rows_y // 4, some, carry)

    lax.fori_loop(first, last, one_row, 0)


def far_matrices(perm_ref, dis_ref, cos_ref, sin_ref, d_ref):
    n_box, rows, _ = d_ref.shape
    n_units = dis_ref.shape[1]
    per_box = rows // n_units
    dis_re, dis_im = dis_ref[0].astype(f32), dis_ref[1].astype(f32)

    def one_box(b, carry):
        for i in range(per_box):
            p = perm_ref[b * per_box + i]
            c = cos_ref[pl.ds(p, 1), :]
            s = sin_ref[pl.ds(p, 1), :]
            d_ref[b, i * n_units : (i + 1) * n_units, :] = jnp.concatenate(
                [c * dis_re - s * dis_im, s * dis_re + c * dis_im], axis=1
            ).astype(bf16)
        return carry

    lax.fori_loop(0, n_box, one_box, 0)


def far_part(slot_ref, lf_ref, d_ref, near_ref, out_ref, far_ref):
    n_sub, n_box, _, quarter, n_sides = lf_ref.shape
    n_patch, n_units, _ = near_ref.shape
    per_box = n_patch // n_box

    def one_box(b):
        field = jnp.concatenate([lf_ref[q, b, c] for c in range(2) for q in range(n_sub)], axis=0)
        far = jnp.dot(d_ref[b], field, preferred_element_type=f32)
        for i in range(per_box):
            far_ref[b * per_box + i] = far[i * n_units : (i + 1) * n_units]

    def two_boxes(h, carry):
        one_box(2 * h)
        one_box(2 * h + 1)
        return carry

    lax.fori_loop(0, n_box // 2, two_boxes, 0)

    def some_patches(h, carry):
        for i in range(8):
            p = h * 8 + i
            out_ref[p] = (near_ref[p] + far_ref[slot_ref[p]]).astype(bf16)
        return carry

    lax.fori_loop(0, n_patch // 8, some_patches, 0)


def fused(
    n_strip, n_sub,
    perm_ref, slot_ref, index_in, cur_in, nb_in, angle_in, agg_in, dis_in, centre_in, shift_in,
    out_ref,
    index_ref, cur_ref, nb_ref, angle_ref, agg_ref, dis_ref, centre_ref, shift_ref, load_sem,
    pad_ref, box_ref, cos_ref, sin_ref, near_ref, a_ref, far_ref, lf_ref,
    cen_ref, shf_ref, in_ref, wide_ref, w_ref, inc_ref, exp_ref, coef_ref, send_ref, d_ref, place_ref, located_ref, place_sem,
    halo_send, halo_recv, cen_send, cen_recv, shf_send, shf_recv, a2a_send, a2a_recv,
    exp_send, exp_recv, back_send, back_recv,
):
    strip = lax.axis_index("strip")
    sub = lax.axis_index("sub")
    rows_x, rows_y = cur_ref.shape[0], cur_ref.shape[1]
    n_units, n_sides = cur_ref.shape[2], cur_ref.shape[3]
    n_patch = rows_x * rows_y
    n_dirs = angle_ref.shape[1]
    quarter = n_dirs // n_sub
    n_box = centre_ref.shape[1]
    all_box = n_box * n_sub
    wide_y = rows_y + 2

    def sub_peer(d):
        return lax.rem(sub + d, n_sub)

    def strip_peer(d):
        return lax.rem(strip + d, n_strip)

    offsets = [(dx, dy) for dx in (-1, 0, 1) for dy in (-1, 0, 1) if dx or dy]

    pairs = [
        (index_in, index_ref), (centre_in, centre_ref), (shift_in, shift_ref), (cur_in, cur_ref),
        (angle_in, angle_ref), (agg_in, agg_ref), (nb_in, nb_ref), (dis_in, dis_ref),
    ]
    loads = [pltpu.make_async_copy(a, b, load_sem.at[i]) for i, (a, b) in enumerate(pairs)]
    for load in loads:
        load.start()

    barrier = pltpu.get_barrier_semaphore()
    for dx in (-1, 1):
        for dy in (-1, 1):
            pl.semaphore_signal(
                barrier, inc=1, device_id=(strip_peer(dx + n_strip), sub_peer(dy + n_sub)), device_id_type=MESH
            )
    for d in range(1, n_sub):
        pl.semaphore_signal(barrier, inc=1, device_id=(strip, sub_peer(d)), device_id_type=MESH)

    def greet(d, carry):
        pl.semaphore_signal(barrier, inc=1, device_id=(strip_peer(d), sub), device_id_type=MESH)
        return carry

    lax.fori_loop(1, n_strip, greet, 0)

    for load in loads[0:3]:
        load.wait()
    cen_ref[sub] = jnp.zeros((8, 128), f32)
    cen_ref[sub, 0:2, 0:n_box] = centre_ref[...]
    wanted = index_ref[...]
    ny_total = rows_y * n_sub
    row = wanted // ny_total
    place = (row - strip * rows_x + 1) * wide_y + (wanted - row * ny_total - sub * rows_y + 1)
    empty = (rows_x + 2) * wide_y
    place = jnp.minimum(jnp.maximum(place, 0), empty)
    place_ref[...] = jnp.where(wanted >= 0, place, empty)
    placing = pltpu.make_async_copy(place_ref, located_ref, place_sem)
    placing.start()
    shf_ref[strip] = jnp.zeros((8, n_dirs), f32)
    shf_ref[strip, 0:2, :] = shift_ref[0]
    pl.semaphore_wait(barrier, 4 + n_sub - 1 + n_strip - 1)

    def cen_copy(d):
        return pltpu.make_async_remote_copy(
            src_ref=cen_ref.at[sub], dst_ref=cen_ref.at[sub],
            send_sem=cen_send.at[d], recv_sem=cen_recv.at[d],
            device_id=(strip, sub_peer(d)), device_id_type=MESH,
        )

    def cen_wait(d):
        src = lax.rem(sub + n_sub - d, n_sub)
        return pltpu.make_async_remote_copy(
            src_ref=cen_ref.at[src], dst_ref=cen_ref.at[src],
            send_sem=cen_send.at[d], recv_sem=cen_recv.at[d],
            device_id=(strip, sub_peer(d)), device_id_type=MESH,
        )

    def strip_copy(buf, send, recv, d, at):
        return pltpu.make_async_remote_copy(
            src_ref=buf.at[at], dst_ref=buf.at[at],
            send_sem=send.at[d], recv_sem=recv.at[d],
            device_id=(strip_peer(d), sub), device_id_type=MESH,
        )

    def halo_copy(n):
        dx, dy = offsets[n]
        src_x = {-1: slice(0, 1), 0: slice(0, rows_x), 1: slice(rows_x - 1, rows_x)}[dx]
        src_y = {-1: slice(0, 1), 0: slice(0, rows_y), 1: slice(rows_y - 1, rows_y)}[dy]
        dst_x = {-1: slice(rows_x + 1, rows_x + 2), 0: slice(1, rows_x + 1), 1: slice(0, 1)}[dx]
        dst_y = {-1: slice(rows_y + 1, rows_y + 2), 0: slice(1, rows_y + 1), 1: slice(0, 1)}[dy]
        return pltpu.make_async_remote_copy(
            src_ref=cur_ref.at[src_x, src_y], dst_ref=pad_ref.at[dst_x, dst_y],
            send_sem=halo_send.at[n], recv_sem=halo_recv.at[n],
            device_id=(strip_peer(dx + n_strip), sub_peer(dy + n_sub)), device_id_type=MESH,
        )

    loads[3].wait()
    for d in range(1, n_sub):
        cen_copy(d).start()

    def send_shift(d, carry):
        strip_copy(shf_ref, shf_send, shf_recv, d, strip).start()
        return carry

    lax.fori_loop(1, n_strip, send_shift, 0)

    loads[4].wait()
    loads[5].wait()
    flat_cur = cur_ref.reshape(n_patch, n_units, n_sides)
    flat_pad = pad_ref.reshape((rows_x + 3) * wide_y, n_units, n_sides)

    gather_boxes(perm_ref, flat_cur, angle_ref, agg_ref, box_ref, cos_ref, sin_ref)

    def a2a_copy(d):
        return pltpu.make_async_remote_copy(
            src_ref=box_ref.at[sub_peer(d)], dst_ref=in_ref.at[d],
            send_sem=a2a_send.at[d], recv_sem=a2a_recv.at[d],
            device_id=(strip, sub_peer(d)), device_id_type=MESH,
        )

    for d in range(1, n_sub):
        a2a_copy(d).start()
    for n in range(len(offsets)):
        halo_copy(n).start()

    for x in range(rows_x):
        pad_ref[x + 1, 1 : rows_y + 1] = cur_ref[x]
    pad_ref[rows_x + 2, 0] = jnp.zeros((n_units, n_sides), bf16)

    def wait_shift(d, carry):
        src = lax.rem(strip + n_strip - d, n_strip)
        strip_copy(shf_ref, shf_send, shf_recv, d, src).wait_recv()
        return carry

    lax.fori_loop(1, n_strip, wait_shift, 0)
    for d in range(1, n_sub):
        cen_wait(d).wait_recv()
    one = jnp.ones((1, n_dirs), f32)
    zero = jnp.zeros((1, n_dirs), f32)

    def times(a, b):
        return a[0] * b[0] - a[1] * b[1], a[0] * b[1] + a[1] * b[0]

    coef = [None] * n_strip
    run = (one, zero)
    for q in reversed(range(n_strip)):
        t = (shf_ref[q, 0:1, :], shf_ref[q, 1:2, :])
        coef[q] = tuple(jnp.where(q < strip, part, 0.0) for part in run)
        run = times((jnp.where(q <= strip, t[0], 1.0), jnp.where(q <= strip, t[1], 0.0)), run)
    run = (one, zero)
    for q in range(n_strip):
        t = (shf_ref[q, 0:1, :], -shf_ref[q, 1:2, :])
        coef[q] = tuple(a + jnp.where(q > strip, part, 0.0) for a, part in zip(coef[q], run))
        run = times((jnp.where(q >= strip, t[0], 1.0), jnp.where(q >= strip, t[1], 0.0)), run)
    stacked = jnp.concatenate([c[0] for c in coef] + [c[1] for c in coef], axis=0)
    coef_ref[...] = stacked.T
    here = coef_ref[pl.ds(pl.multiple_of(sub * quarter, quarter), quarter), :]

    cen_row = jnp.concatenate([cen_ref[i, :, 0:n_box] for i in range(n_sub)], axis=1)
    cen_col = jnp.concatenate([cen_ref[i].T[0:n_box, :] for i in range(n_sub)], axis=0)
    col_x, col_y = cen_col[:, 0:1], cen_col[:, 1:2]
    row_x, row_y = cen_row[0:1, :], cen_row[1:2, :]
    step = 2.0 * math.pi / n_dirs
    k_col = lax.broadcasted_iota(jnp.int32, (quarter, all_box), 0) + sub * quarter
    angle = k_col.astype(f32) * step
    mid_x = (strip.astype(f32) + 0.5) * rows_x
    mid_y = 0.5 * rows_y * n_sub
    psi = wave_number * ((row_x - mid_x) * jnp.cos(angle) + (row_y - mid_y) * jnp.sin(angle))
    psi_re, psi_im = jnp.cos(psi), jnp.sin(psi)

    fold = 128 // all_box
    dx = col_x - jnp.concatenate([row_x] * fold, axis=1)
    dy = col_y - jnp.concatenate([row_y] * fold, axis=1)
    rho = jnp.sqrt(dx * dx + dy * dy)
    lane = lax.broadcasted_iota(jnp.int32, (all_box, 128), 1)
    target = lax.broadcasted_iota(jnp.int32, (all_box, 128), 0)
    amplitude = jnp.where(lane % all_box != target, 1.0 / (1.0 + rho), 0.0)
    lane_k = lax.broadcasted_iota(jnp.int32, (1, 128), 1) // all_box

    def weights(g, carry):
        turn = (lane_k + g * fold + sub * quarter).astype(f32) * step
        arg = wave_number * (rho + jnp.cos(turn) * dx + jnp.sin(turn) * dy)
        w_re = (amplitude * jnp.cos(arg)).astype(bf16).astype(f32)
        w_im = (amplitude * jnp.sin(arg)).astype(bf16).astype(f32)
        for i in range(fold):
            part = slice(i * all_box, (i + 1) * all_box)
            a, b = w_re[:, part], w_im[:, part]
            w_ref[g * fold + i] = jnp.concatenate(
                [jnp.concatenate([a, -b], axis=1), jnp.concatenate([b, a], axis=1)], axis=0
            ).astype(bf16)
        return carry

    lax.fori_loop(0, quarter // fold, weights, 0)

    placing.wait()
    loads[6].wait()
    loads[7].wait()
    far_matrices(perm_ref, dis_ref, cos_ref, sin_ref, d_ref)

    def source(d):
        return lax.rem(sub + n_sub - d, n_sub)

    for d in range(n_sub):
        if d:
            a2a_copy(d).wait_recv()
        base = source(d)
        for b in range(n_box):
            for c in range(2):
                block = box_ref[sub, b, c] if d == 0 else in_ref[d, b, c]
                at = (c * all_box + base * n_box + b) * quarter
                wide_ref[pl.ds(pl.multiple_of(at, quarter), quarter), :] = block.astype(f32)

    total_re = jnp.zeros((quarter, n_sides), f32)
    total_im = jnp.zeros((quarter, n_sides), f32)
    for b in range(all_box):
        p_re, p_im = psi_re[:, b : b + 1], psi_im[:, b : b + 1]
        v_re = wide_ref[b * quarter : (b + 1) * quarter, :]
        v_im = wide_ref[(all_box + b) * quarter : (all_box + b + 1) * quarter, :]
        total_re += p_re * v_re - p_im * v_im
        total_im += p_im * v_re + p_re * v_im
    exp_ref[strip, 0] = (strip_weight * total_re).astype(bf16)
    exp_ref[strip, 1] = (strip_weight * total_im).astype(bf16)

    def send_exp(d, carry):
        strip_copy(exp_ref, exp_send, exp_recv, d, strip).start()
        return carry

    lax.fori_loop(1, n_strip, send_exp, 0)

    def interact(g, carry):
        ks = [g * 8 + i for i in range(8)]
        rhs = [wide_ref[pl.ds(k, 2 * all_box, stride=quarter), :].astype(bf16) for k in ks]
        out = [jnp.dot(w_ref[k], v, preferred_element_type=f32) for k, v in zip(ks, rhs)]
        for k, v in zip(ks, out):
            inc_ref[pl.ds(k, 2 * all_box, stride=quarter), :] = v
        return carry

    lax.fori_loop(0, quarter // 8, interact, 0)

    def wait_exp(d, carry):
        src = lax.rem(strip + n_strip - d, n_strip)
        strip_copy(exp_ref, exp_send, exp_recv, d, src).wait_recv()
        return carry

    lax.fori_loop(1, n_strip, wait_exp, 0)
    field_re = jnp.zeros((quarter, n_sides), f32)
    field_im = jnp.zeros((quarter, n_sides), f32)
    for q in range(n_strip):
        c_re, c_im = here[:, q : q + 1], here[:, n_strip + q : n_strip + q + 1]
        v_re, v_im = exp_ref[q, 0].astype(f32), exp_ref[q, 1].astype(f32)
        field_re += c_re * v_re - c_im * v_im
        field_im += c_re * v_im + c_im * v_re
    def back_copy(d, at, to):
        return pltpu.make_async_remote_copy(
            src_ref=send_ref.at[to], dst_ref=lf_ref.at[at],
            send_sem=back_send.at[d], recv_sem=back_recv.at[d],
            device_id=(strip, to), device_id_type=MESH,
        )

    for b in range(all_box):
        p_re, p_im = psi_re[:, b : b + 1], psi_im[:, b : b + 1]
        v_re = inc_ref[b * quarter : (b + 1) * quarter, :]
        v_im = inc_ref[(all_box + b) * quarter : (all_box + b + 1) * quarter, :]
        send_ref[b // n_box, b % n_box, 0] = (v_re + p_re * field_re + p_im * field_im).astype(bf16)
        send_ref[b // n_box, b % n_box, 1] = (v_im + p_re * field_im - p_im * field_re).astype(bf16)
        if b % n_box == n_box - 1:
            to = b // n_box

            @pl.when(to != sub)
            def _(to=to):
                back_copy(lax.rem(to - sub + n_sub, n_sub), sub, to).start()


    lf_ref[sub] = send_ref[sub]

    for n in range(len(offsets)):
        halo_copy(n).wait_recv()
    near_part(0, rows_x, located_ref, nb_ref, flat_pad, near_ref, a_ref)

    for d in range(1, n_sub):
        back_copy(d, source(d), sub_peer(d)).wait_recv()
    far_part(slot_ref, lf_ref, d_ref, near_ref, out_ref, far_ref)

    for d in range(1, n_sub):
        cen_copy(d).wait_send()
        a2a_copy(d).wait_send()
        back_copy(d, sub, sub_peer(d)).wait_send()

    def drain(d, carry):
        strip_copy(shf_ref, shf_send, shf_recv, d, strip).wait_send()
        strip_copy(exp_ref, exp_send, exp_recv, d, strip).wait_send()
        return carry

    lax.fori_loop(1, n_strip, drain, 0)
    for n in range(len(offsets)):
        halo_copy(n).wait_send()


def per_device(
    currents,
    near_blocks,
    near_index,
    box_of_patch,
    box_centre,
    patch_angle,
    aggregation,
    disaggregation,
    strip_shift,
):
    rows_x, rows_y, n_units, n_sides = currents.shape
    n_dirs = patch_angle.shape[2]
    n_slots = near_index.shape[2]
    n_patch = rows_x * rows_y
    box_dev = box_centre.shape[0]
    n_sub = lax.axis_size("sub")
    n_strip = lax.axis_size("strip")
    quarter = n_dirs // n_sub
    all_box = box_dev * n_sub
    ids = jnp.arange(n_patch, dtype=jnp.int32)
    key = box_of_patch.reshape(n_patch) * n_patch + ids
    slot = jnp.sum((key[None, :] < key[:, None]).astype(jnp.int32), axis=1)
    perm = jnp.sum(jnp.where(slot[None, :] == ids[:, None], ids[None, :], 0), axis=1)
    smem = pl.BlockSpec(memory_space=pltpu.SMEM)
    vmem = pl.BlockSpec(memory_space=pltpu.VMEM)
    dma = pltpu.SemaphoreType.DMA
    operands = (
        jnp.transpose(near_index, (2, 0, 1)),
        currents,
        jnp.transpose(near_blocks, (0, 2, 1, 3)),
        patch_angle.reshape(n_patch, n_dirs),
        jnp.swapaxes(aggregation, 1, 2),
        jnp.swapaxes(disaggregation, 1, 2),
        box_centre.T,
        strip_shift,
    )
    hbm = pl.BlockSpec(memory_space=pltpu.HBM)
    scratch = [pltpu.VMEM(a.shape, a.dtype) for a in operands] + [
        dma((8,)),
        pltpu.VMEM((rows_x + 3, rows_y + 2, n_units, n_sides), bf16),
        pltpu.VMEM((n_sub, box_dev, 2, quarter, n_sides), bf16),
        pltpu.VMEM((n_patch, n_dirs), f32),
        pltpu.VMEM((n_patch, n_dirs), f32),
        pltpu.VMEM((n_patch, n_units, n_sides), f32),
        pltpu.VMEM((n_slots * 8 * rows_y, 128), f32),
        pltpu.VMEM((n_patch, n_units, n_sides), f32),
        pltpu.VMEM((n_sub, box_dev, 2, quarter, n_sides), bf16),
        pltpu.VMEM((n_sub, 8, 128), f32),
        pltpu.VMEM((n_strip, 8, n_dirs), f32),
        pltpu.VMEM((n_sub, box_dev, 2, quarter, n_sides), bf16),
        pltpu.VMEM((2 * all_box * quarter, n_sides), f32),
        pltpu.VMEM((quarter, 2 * all_box, 2 * all_box), bf16),
        pltpu.VMEM((2 * all_box * quarter, n_sides), f32),
        pltpu.VMEM((n_strip, 2, quarter, n_sides), bf16),
        pltpu.VMEM((n_dirs, 2 * n_strip), f32),
        pltpu.VMEM((n_sub, box_dev, 2, quarter, n_sides), bf16),
        pltpu.VMEM((box_dev, n_patch // box_dev * n_units, 2 * n_dirs), bf16),
        pltpu.VMEM((n_slots, rows_x, rows_y), jnp.int32),
        pltpu.SMEM((n_slots, rows_x, rows_y), jnp.int32),
        dma(()),
        dma((8,)), dma((8,)),
        dma((n_sub,)), dma((n_sub,)),
        dma((n_strip,)), dma((n_strip,)),
        dma((n_sub,)), dma((n_sub,)),
        dma((n_strip,)), dma((n_strip,)),
        dma((n_sub,)), dma((n_sub,)),
    ]
    result = pl.pallas_call(
        functools.partial(fused, n_strip, n_sub),
        out_shape=jax.ShapeDtypeStruct((n_patch, n_units, n_sides), bf16),
        in_specs=[smem] * 2 + [hbm] * 8,
        out_specs=vmem,
        scratch_shapes=scratch,
        compiler_params=pltpu.CompilerParams(
            collective_id=0, has_side_effects=True, vmem_limit_bytes=60 * 1024 * 1024
        ),
    )(
        perm,
        slot,
        *operands,
    )
    return result.reshape(rows_x, rows_y, n_units, n_sides)


def solution(mesh):
    in_specs = (
        P("strip", "sub", None, None),
        P("strip", "sub", None, None),
        P("strip", "sub", None),
        P("strip", "sub"),
        P(("strip", "sub"), None),
        P("strip", "sub", None),
        P(),
        P(),
        P("strip", None, None),
    )
    out_specs = P("strip", "sub", None, None)
    return jax.shard_map(
        per_device, mesh=mesh, in_specs=in_specs, out_specs=out_specs, check_vma=False
    )
```
